32 devices in a mesh: dp: 16 (over z, x, core), mp: 2 (over y).
Axes of the slice: x: 2, y: 2, z: 4, core: 2. Of those that a mesh axis runs over, the one named last changes fastest.
Arguments:
- frames_in: bfloat16 [8, 4096, 1024], P('mp', 'dp'), may hold values from -6 to 6
- delays: int32 [8], P('mp'), may hold values from 1 to 2, as said below
- item_bounds: int32 [2], replicated, may hold values from 1 to 4095, as said below
- attn_gain: float32 [8, 1024], P('mp'), may hold values from 0.1 to 1.9
- ffn_gain: float32 [8, 1024], P('mp'), may hold values from 0.1 to 1.9
- w_qkv: bfloat16 [8, 3, 1024, 1024], P(None, None, None, 'mp'), may hold values from -0.1875 to 0.1875
- w_out: bfloat16 [8, 1024, 1024], P(None, None, 'mp'), may hold values from -0.375 to 0.375
- w_gate_up: bfloat16 [8, 2, 1024, 2816], P(None, None, None, 'mp'), may hold values from -0.1875 to 0.1875
- w_down: bfloat16 [8, 1024, 2816], P(None, None, 'mp'), may hold values from -0.15625 to 0.15625
- cotangent: bfloat16 [8, 4096, 1024], P('mp', 'dp'), may hold values from -6 to 6
Outputs:
- mixed: bfloat16 [8, 4096, 1024], P('mp', 'dp')
- input_grad: float32 [8, 4096, 1024], P('mp', 'dp')
- attn_gain_grad: float32 [8, 1024], P('mp', 'dp')
- ffn_gain_grad: float32 [8, 1024], P('mp', 'dp')
- qkv_grad: float32 [8, 3, 1024, 1024], P(None, None, 'dp', 'mp')
- out_grad: float32 [8, 1024, 1024], P(None, 'dp', 'mp')
- gate_up_grad: float32 [8, 2, 1024, 2816], P(None, None, 'dp', 'mp')
- down_grad: float32 [8, 1024, 2816], P(None, 'dp', 'mp')
The draws below stay inside these ranges and needn't reach their ends.
Inputs may be any that keep to these rules, and one draw needn't show every extreme that they name: Each position is delayed by 1 or 2 frames, and both delays occur. item_bounds[0] lies among the first 256 frames and item_bounds[1] among the last 256; items begin at frame 0 and at each bound.
All inputs are finite; a program needn't handle non-finite values.
Results may differ from the reference program's by a relative error of at most 0.012.
Values may be sent and summed in bfloat16 or wider, within the bound.
A program may use at most 640 MiB of HBM per device.

```python
import math
import jax
import jax.numpy as jnp
from jax import lax

D = 1024
H = 16
HD = 64
FF = 2816
POS = 8
FR_DEV = 256
FRAMES = 4096


def draw_delays(key, part):
    key = jax.random.fold_in(key, 11)
    lag_values = jax.random.randint(jax.random.fold_in(key, 1), (POS,), 1, 3)
    ordering = jax.random.permutation(jax.random.fold_in(key, 2), POS)
    places = jnp.arange(POS)
    lag_values = jnp.where(places == ordering[0], 2, lag_values)
    lag_values = jnp.where(places == ordering[1], 1, lag_values)
    return lag_values.astype(jnp.int32)


def draw_item_bounds(key, part):
    key = jax.random.fold_in(key, 23)
    first_bound = jax.random.randint(jax.random.fold_in(key, 1), (1,), 1, FR_DEV)
    second_bound = FRAMES - jax.random.randint(jax.random.fold_in(key, 2), (1,), 1, FR_DEV)
    return jnp.concatenate([first_bound, second_bound]).astype(jnp.int32)


def with_spikes(values, stream_key, source, target, blocks, factor):
    owner, partner = [(jnp.arange(values.shape[position]) // (values.shape[position] // blocks)).reshape([-1 if axis == position else 1 for axis in range(values.ndim)]) for position in (source, target)]
    chosen = jax.random.permutation(stream_key, blocks)[partner]
    strong = (owner == chosen) | (owner == (partner + blocks // 2) % blocks)
    return jnp.where(strong, factor * values, values)


def shard_levels(key, extent, pieces, smallest, top_value):
    factor_of = 1.0
    for axis_at, shards_of in pieces:
        heights = jax.random.uniform(jax.random.fold_in(jax.random.fold_in(key, 6), axis_at), (shards_of,), jnp.float32, smallest / len(pieces), top_value / len(pieces))
        factor_of = factor_of * jnp.repeat(jnp.exp(heights), extent[axis_at] // shards_of).reshape((-1,) + (1,) * (len(extent) - 1 - axis_at))
    return factor_of


def gaussian(own_key, dims, scale, reach, shards=(), kind=jnp.bfloat16):
    loudness = shard_levels(own_key, dims, shards, -0.22, 0.18) if shards else 1.0
    result = jax.random.normal(own_key, dims, jnp.float32) * scale * loudness
    return jnp.minimum(jnp.maximum(result, -reach), reach).astype(kind)


def gaussian_with(own_key, shape, scale, limit, cuts, heavy, held_as=jnp.bfloat16):
    result = scale * jax.random.normal(own_key, shape, jnp.float32)
    if cuts:
        result = result * shard_levels(own_key, shape, cuts, -0.22, 0.18)
    return jnp.clip(with_spikes(result, jax.random.fold_in(own_key, 3), *heavy), -limit, limit).astype(held_as)


def setup_inputs(seed: int = 0) -> dict:
    key_list = jax.random.split(jax.random.key(seed), 11)
    frames_in = gaussian(key_list[0], (POS, FRAMES, D), 1.0, 6.0, ((0, 2), (1, 16)))
    delays = draw_delays(jax.random.fold_in(key_list[10], 71), 0)
    item_bounds = draw_item_bounds(jax.random.fold_in(key_list[10], 71), 0)
    attn_gain = jnp.clip(1.0 + 0.18 * jax.random.normal(key_list[3], (POS, D), jnp.float32), 0.1, 1.9)
    ffn_gain = jnp.clip(1.0 + 0.18 * jax.random.normal(key_list[4], (POS, D), jnp.float32), 0.1, 1.9)
    w_qkv = gaussian(key_list[5], (POS, 3, D, H * HD), D ** -0.5, 0.1875, ((3, 2),))
    w_out = gaussian(key_list[6], (POS, D, H * HD), (H * HD // 4) ** -0.5, 0.375, ((2, 2),))
    w_gate_up = gaussian(key_list[7], (POS, 2, D, FF), D ** -0.5, 0.1875, ((3, 2),))
    w_down = gaussian(key_list[8], (POS, D, FF), (FF // 2) ** -0.5, 0.15625, ((2, 2),))
    cotangent = gaussian_with(key_list[9], (POS, FRAMES, D), 1.0, 6.0, ((0, 2), (1, 16)), (1, 2, 16, 2.0))
    return dict(frames_in=frames_in, delays=delays, item_bounds=item_bounds, attn_gain=attn_gain, ffn_gain=ffn_gain, w_qkv=w_qkv, w_out=w_out, w_gate_up=w_gate_up, w_down=w_down, cotangent=cotangent)


epsilon = 1e-05
highest = lax.Precision.HIGHEST

@jax.custom_vjp
def low(v):
    return lax.optimization_barrier(v.astype(jnp.bfloat16)).astype(jnp.float32)

@jax.custom_vjp
def low_back(v):
    return v

def low_keep(v):
    return (low(v), None)

def low_pass(kept, grad):
    return (grad,)

def back_keep(v):
    return (v, None)

def back_low(kept, grad):
    return (low(grad),)
low.defvjp(low_keep, low_pass)
low_back.defvjp(back_keep, back_low)

def normalize(values, gain):
    return values * lax.rsqrt(lax.optimization_barrier(jnp.mean(values * values, axis=-1, keepdims=True)) + epsilon) * gain[:, None, :]

def delay_frames(frames_in, delays, item_bounds):
    frame_count = frames_in.shape[1]
    padded = jnp.pad(frames_in, ((0, 0), (2, 0), (0, 0)))

    def take_frames(frame_row, shift_lag):
        return lax.dynamic_slice_in_dim(frame_row, (2 - shift_lag).astype(jnp.int32), frame_count, 0)
    shifted = jax.vmap(take_frames)(padded, delays)
    frame_ids = jnp.arange(frame_count, dtype=jnp.int32)
    item_start = jnp.where(frame_ids >= item_bounds[1], item_bounds[1], jnp.where(frame_ids >= item_bounds[0], item_bounds[0], 0))
    usable = frame_ids[None, :] - delays[:, None] >= item_start[None, :]
    return jnp.where(usable[:, :, None], shifted, jnp.zeros_like(shifted))

def layer_block(resid, attn_gain, ffn_gain, w_qkv, w_out, w_gate_up, w_down):
    positions, frame_count, model_width = resid.shape
    normed_a = low(normalize(resid, attn_gain))
    qkv = low_back(low(jnp.einsum('pfd,pcde->pcfe', normed_a, w_qkv, precision=highest)))
    split = qkv.reshape(positions, 3, frame_count, H, HD)
    queries, key_rows, values = (split[:, 0], split[:, 1], split[:, 2])
    scores = low_back(jnp.einsum('ifhe,jfhe->fhij', queries, key_rows, precision=highest) * 0.125)
    causal = jnp.tril(jnp.ones((positions, positions), dtype=bool))
    scores = jnp.where(causal, scores, -1e+30)
    probs = low(jax.nn.softmax(scores, axis=-1))
    context = jnp.einsum('fhij,jfhe->ifhe', probs, values, precision=highest).reshape(positions, frame_count, H * HD)
    context = low_back(low(context))
    attn_part = low_back(jnp.einsum('pfe,pde->pfd', context, w_out, precision=highest))
    middle = resid + attn_part
    normed_f = low(normalize(middle, ffn_gain))
    gate_up = low_back(jnp.einsum('pfd,pcdh->pcfh', normed_f, w_gate_up, precision=highest))
    hidden = low(jax.nn.silu(gate_up[:, 0]) * gate_up[:, 1])
    return middle + jnp.einsum('pfh,pdh->pfd', hidden, w_down, precision=highest)

def forward(frames_in, attn_gain, ffn_gain, w_qkv, w_out, w_gate_up, w_down, delays, item_bounds):
    resid = delay_frames(frames_in, delays, item_bounds)
    positions, frame_count, model_width = resid.shape
    block_frames = math.gcd(frame_count, 512)
    block_count = frame_count // block_frames
    blocks = resid.reshape(positions, block_count, block_frames, model_width).transpose(1, 0, 2, 3)
    one_block = jax.checkpoint(lambda block_rows: layer_block(block_rows, attn_gain, ffn_gain, w_qkv, w_out, w_gate_up, w_down))

    def step_block(carry, block_rows):
        return (carry, one_block(block_rows))
    unused, outputs = lax.scan(step_block, jnp.zeros((), jnp.float32), blocks)
    return outputs.transpose(1, 0, 2, 3).reshape(positions, frame_count, model_width)

def reference(frames_in, delays, item_bounds, attn_gain, ffn_gain, w_qkv, w_out, w_gate_up, w_down, cotangent):
    inputs = (frames_in.astype(jnp.float32), attn_gain.astype(jnp.float32), ffn_gain.astype(jnp.float32), w_qkv.astype(jnp.float32), w_out.astype(jnp.float32), w_gate_up.astype(jnp.float32), w_down.astype(jnp.float32))

    def apply_layer(frames_val, gain_a, gain_f, wq_val, wo_val, wgu_val, wd_val):
        return forward(frames_val, gain_a, gain_f, wq_val, wo_val, wgu_val, wd_val, delays, item_bounds)
    primal, pullback = jax.vjp(apply_layer, *inputs)
    grads = pullback(cotangent.astype(jnp.float32))
    return (primal.astype(jnp.bfloat16), grads[0], grads[1], grads[2], grads[3], grads[4], grads[5], grads[6])
```

```python
import functools

import jax
import jax.numpy as jnp
from jax import lax
from jax.experimental import pallas as pl
from jax.experimental.pallas import tpu as pltpu
from jax.sharding import PartitionSpec as P

HD = 64
EPSILON = 1e-05
BF16 = jnp.bfloat16
F32 = jnp.float32


def shift_frames(block, distance):
    devices = range(lax.axis_size("dp"))
    route = [(i - distance, i) for i in devices if i - distance in devices]
    return lax.ppermute(block, "dp", route)


def at(array, index, axis=0):
    return lax.dynamic_index_in_dim(array, index, axis, keepdims=False)


class Group:
    def __init__(self, positions, local_pos):
        self.dp, self.mp = lax.axis_size("dp"), lax.axis_size("mp")
        power = local_pos & (local_pos - 1) == 0
        self.size = local_pos if power and self.dp % local_pos == 0 else 1
        self.outer = self.dp // self.size
        self.member = lax.axis_index("dp") % self.size
        self.m = lax.axis_index("mp")

    def swap(self, block):
        return lax.ppermute(block, "mp", [(0, 1), (1, 0)])

    def gather(self, block):
        if self.mp != 2:
            return lax.all_gather(block, "mp", axis=0)
        other = self.swap(block)
        first = self.m == 0
        return jnp.stack([jnp.where(first, block, other), jnp.where(first, other, block)])

    def scatter(self, blocks):
        if self.mp != 2:
            return lax.psum_scatter(blocks, "mp", scatter_dimension=0, tiled=False)
        other = self.swap(at(blocks, 1 - self.m).astype(BF16))
        return at(blocks, self.m) + other.astype(F32)

    def route(self, step):
        return [(i, i ^ step) for i in range(self.dp)]

    def spread(self, blocks):
        got = [at(blocks, self.member)]
        for step in range(1, self.size):
            got.append(lax.ppermute(at(blocks, self.member ^ step), "dp", self.route(step)))
        return jnp.stack(got)

    def unspread(self, blocks):
        got = [blocks[0]]
        for step in range(1, self.size):
            got.append(lax.ppermute(blocks[step], "dp", self.route(step)))
        return self.in_order(jnp.stack(got))

    def in_order(self, blocks):
        bit = 1
        while bit < self.size:
            flipped = blocks.reshape((self.size // (2 * bit), 2, bit) + blocks.shape[1:])[:, ::-1]
            flipped = flipped.reshape(blocks.shape)
            blocks = jnp.where((self.member & bit) != 0, flipped, blocks)
            bit *= 2
        return blocks

    def by_position(self, blocks):
        got = self.spread(jnp.swapaxes(blocks, 0, 1))
        return jnp.swapaxes(got, 0, 1).reshape(self.mp, -1, blocks.shape[-1])

    def sum_scatter(self, values):
        dp = self.dp
        if dp & (dp - 1):
            return lax.psum_scatter(
                values, "dp", scatter_dimension=values.ndim - 1, tiled=True
            )
        me = lax.axis_index("dp")
        bit = dp // 2
        while bit:
            halves = values.reshape(values.shape[:-1] + (2, values.shape[-1] // 2))
            high = (me & bit) != 0
            keep = jnp.where(high, halves[..., 1, :], halves[..., 0, :])
            give = jnp.where(high, halves[..., 0, :], halves[..., 1, :])
            values = keep + lax.ppermute(give, "dp", self.route(bit))
            bit //= 2
        return values


def grad_kernel(left, right, out):
    out[0, 0, 0] = lax.dot_general(
        left[0], right[0, 0], (((0,), (0,)), ((), ())), preferred_element_type=F32
    ).astype(BF16)


def weight_grad(left, right, outer):
    groups, rows, depth = left.shape
    parts, width = right.shape[1], right.shape[3]
    block = depth // outer
    if block % 128:
        full = jnp.einsum("mrd,mcrn->mcdn", left, right, preferred_element_type=F32).astype(BF16)
        return full.reshape(groups, parts, outer, block, width).transpose(2, 0, 1, 3, 4)
    return pl.pallas_call(
        grad_kernel,
        grid=(groups, parts, outer),
        in_specs=[
            pl.BlockSpec((1, rows, block), lambda m, c, o: (m, 0, o)),
            pl.BlockSpec((1, 1, rows, width), lambda m, c, o: (m, c, 0, 0)),
        ],
        out_specs=pl.BlockSpec((1, 1, 1, block, width), lambda m, c, o: (o, m, c, 0, 0)),
        out_shape=jax.ShapeDtypeStruct((outer, groups, parts, block, width), BF16),
        compiler_params=pltpu.CompilerParams(vmem_limit_bytes=48 * 1024 * 1024),
        cost_estimate=pl.CostEstimate(
            flops=2 * groups * parts * rows * depth * width,
            bytes_accessed=2 * groups * (rows * depth + parts * width * (rows + depth)),
            transcendentals=0,
        ),
        name="weight_grad",
    )(left, right)


def normalize(values, gain):
    scale = lax.rsqrt(jnp.mean(values * values, axis=-1, keepdims=True) + EPSILON)
    return values * scale * gain[:, None, :], scale


def norm_back(values, scale, gain, upstream):
    gained = gain[:, None, :] * upstream
    gain_grad = jnp.sum(upstream * values * scale, axis=1)
    value_grad = scale * gained - values * (scale * scale * scale) * jnp.mean(
        gained * values, axis=-1, keepdims=True
    )
    return value_grad, gain_grad


def local(
    frames_in, delays, item_bounds, attn_gain, ffn_gain, w_qkv, w_out, w_gate_up, w_down, cotangent
):
    local_pos, frames, width = frames_in.shape
    positions, head_width = w_qkv.shape[0], w_qkv.shape[3]
    heads = head_width // HD
    group = Group(positions, local_pos)
    mp, size, outer = group.mp, group.size, group.outer
    if size == local_pos:
        mine = lambda w: at(w.reshape((mp, size) + w.shape[1:]), group.member, 1)
    rest = local_pos // size

    frame_ids = lax.axis_index("dp") * frames + jnp.arange(frames, dtype=jnp.int32)
    earlier = shift_frames(frames_in[:, frames - 2 :, :], 1)
    padded = jnp.concatenate([earlier, frames_in], axis=1)
    one = (delays == 1)[:, None, None]
    shifted = jnp.where(one, padded[:, 1 : frames + 1], padded[:, :frames])
    item_start = jnp.where(
        frame_ids >= item_bounds[1],
        item_bounds[1],
        jnp.where(frame_ids >= item_bounds[0], item_bounds[0], 0),
    )
    usable = frame_ids[None, :] - delays[:, None] >= item_start[None, :]
    resid = jnp.where(usable[:, :, None], shifted.astype(F32), 0.0)

    normed_a, scale_a = normalize(resid, attn_gain)
    normed_all = group.gather(normed_a.astype(BF16)).reshape(positions, frames, width)
    qkv = jnp.einsum("pfd,pcde->pcfe", normed_all, w_qkv, preferred_element_type=F32).astype(BF16)
    split = qkv.reshape(positions, 3, frames, heads, HD)
    queries, key_rows, values = (split[:, 0], split[:, 1], split[:, 2])
    scores = jnp.einsum("ifhe,jfhe->fhij", queries, key_rows, preferred_element_type=F32) * 0.125
    causal = jnp.tril(jnp.ones((positions, positions), dtype=bool))
    scores = jnp.where(causal, scores, -1e30)
    probs = jax.nn.softmax(scores, axis=-1)
    probs_low = probs.astype(BF16)
    context = jnp.einsum("fhij,jfhe->ifhe", probs_low, values, preferred_element_type=F32)
    context = context.astype(BF16).reshape(positions, frames, head_width)
    attn_part = jnp.einsum("pfe,pde->pfd", context, w_out, preferred_element_type=F32)
    middle = resid + group.scatter(attn_part.reshape(mp, local_pos, frames, width))

    normed_f, scale_f = normalize(middle, ffn_gain)
    rows = size * frames
    cot_rows = group.gather(group.spread(cotangent).reshape(rows, width))
    ffn_rows = group.gather(group.spread(normed_f.astype(BF16)).reshape(rows, width))
    up_weights, down_weights = mine(w_gate_up), mine(w_down)
    gate_up = jnp.einsum("mrd,mcdn->mcrn", ffn_rows, up_weights, preferred_element_type=F32)
    gate, up = gate_up[:, 0], gate_up[:, 1]
    sigma = jax.nn.sigmoid(gate)
    hidden = (gate * sigma * up).astype(BF16)
    down_part = weight_grad(cot_rows, hidden[:, None], outer)
    d_hidden = jnp.einsum("mrd,mdn->mrn", cot_rows, down_weights, preferred_element_type=F32)
    d_gate = d_hidden * up * sigma * (1.0 + gate * (1.0 - sigma))
    d_up = d_hidden * gate * sigma
    d_gate_up = jnp.stack([d_gate, d_up], axis=1).astype(BF16)
    gate_up_part = weight_grad(ffn_rows, d_gate_up, outer)
    d_rows = group.scatter(
        jnp.einsum("mcrn,mcdn->mrd", d_gate_up, up_weights, preferred_element_type=F32)
    ).astype(BF16)
    d_normed_f = group.unspread(d_rows.reshape(size, frames, width)).astype(F32)
    out_rows = group.scatter(
        jnp.einsum("mrn,mdn->mrd", hidden, down_weights, preferred_element_type=F32)
    ).astype(BF16)
    mixed = (
        middle + group.unspread(out_rows.reshape(size, frames, width)).astype(F32)
    ).astype(BF16)

    middle_grad, ffn_gain_part = norm_back(middle, scale_f, ffn_gain, d_normed_f)
    d_middle = cotangent.astype(F32) + middle_grad
    d_middle_all = group.gather(d_middle.astype(BF16)).reshape(positions, frames, width)
    d_context = jnp.einsum("pfd,pde->pfe", d_middle_all, w_out, preferred_element_type=F32)
    d_context = d_context.astype(BF16).reshape(positions, frames, heads, HD)
    d_probs = jnp.einsum("ifhe,jfhe->fhij", d_context, values, preferred_element_type=F32)
    d_values = jnp.einsum("fhij,ifhe->jfhe", probs_low, d_context, preferred_element_type=F32)
    d_scores = (probs * (d_probs - jnp.sum(probs * d_probs, axis=-1, keepdims=True))).astype(BF16)
    d_queries = jnp.einsum("fhij,jfhe->ifhe", d_scores, key_rows, preferred_element_type=F32)
    d_keys = jnp.einsum("fhij,ifhe->jfhe", d_scores, queries, preferred_element_type=F32)
    d_qkv = jnp.stack([d_queries * 0.125, d_keys * 0.125, d_values], axis=1)
    d_qkv = d_qkv.reshape(positions, 3, frames, head_width).astype(BF16)
    d_normed_a = group.scatter(
        jnp.einsum("pcfe,pcde->pfd", d_qkv, w_qkv, preferred_element_type=F32).reshape(
            mp, local_pos, frames, width
        )
    )
    by_pos = lambda v: group.by_position(v.reshape((mp, size, frames, v.shape[-1])))
    context_rows, d_middle_rows, normed_rows = by_pos(context), by_pos(d_middle_all), by_pos(normed_all)
    d_qkv_rows = jnp.stack([by_pos(d_qkv[:, c]) for c in range(3)], axis=1)
    out_part = weight_grad(d_middle_rows, context_rows[:, None], outer)
    qkv_part = weight_grad(normed_rows, d_qkv_rows, outer)

    resid_grad, attn_gain_part = norm_back(resid, scale_a, attn_gain, d_normed_a)
    d_resid = d_middle + resid_grad
    spread = jnp.where(usable[:, :, None], d_resid, 0.0)
    blank = jnp.zeros((local_pos, 1, width), F32)
    placed = jnp.where(
        one,
        jnp.concatenate([blank, spread, blank], axis=1),
        jnp.concatenate([spread, blank, blank], axis=1),
    )
    returned = shift_frames(placed[:, :2, :], -1)
    input_grad = placed[:, 2:, :] + jnp.pad(returned, ((0, 0), (frames - 2, 0), (0, 0)))

    lines = [[o * size + k for o in range(outer)] for k in range(size)]

    def finish(part):
        whole = lax.psum_scatter(
            part, "dp", scatter_dimension=0, axis_index_groups=lines, tiled=True
        )[0]
        groups, parts, depth, n = whole.shape
        whole = whole.reshape(groups, parts, size, depth // size, n).transpose(2, 0, 1, 3, 4)
        got = group.in_order(group.spread(whole))
        return got.transpose(1, 0, 2, 3, 4).reshape(positions, parts, depth // size, n).astype(F32)

    down_grad = finish(down_part)[:, 0]
    gate_up_grad = finish(gate_up_part)
    out_grad = finish(out_part)[:, 0]
    qkv_grad = finish(qkv_part)
    attn_gain_grad, ffn_gain_grad = group.sum_scatter(jnp.stack([attn_gain_part, ffn_gain_part]))
    return (
        mixed,
        input_grad,
        attn_gain_grad,
        ffn_gain_grad,
        qkv_grad,
        out_grad,
        gate_up_grad,
        down_grad,
    )


def solution(mesh):
    placed = (
        P("mp", "dp", None),
        P("mp"),
        P(),
        P("mp", None),
        P("mp", None),
        P(None, None, None, "mp"),
        P(None, None, "mp"),
        P(None, None, None, "mp"),
        P(None, None, "mp"),
        P("mp", "dp", None),
    )
    return jax.shard_map(
        local,
        mesh=mesh,
        in_specs=placed,
        out_specs=(
            P("mp", "dp", None),
            P("mp", "dp", None),
            P("mp", "dp"),
            P("mp", "dp"),
            P(None, None, "dp", "mp"),
            P(None, "dp", "mp"),
            P(None, None, "dp", "mp"),
            P(None, "dp", "mp"),
        ),
        check_vma=False,
    )
```

```python
import functools

import jax
import jax.numpy as jnp
from jax import lax
from jax.experimental import pallas as pl
from jax.experimental.pallas import tpu as pltpu
from jax.sharding import PartitionSpec as P

HD = 64
LANES = 128
EPSILON = 1e-05
BF16 = jnp.bfloat16
F32 = jnp.float32
MIB = 1024 * 1024
WEIGHT = 100


def dot(left, right, contract):
    return lax.dot_general(left, right, ((contract[:1], contract[1:]), ((), ())), preferred_element_type=F32)


def shift_frames(block, distance):
    devices = range(lax.axis_size("dp"))
    route = [(i - distance, i) for i in devices if i - distance in devices]
    return lax.ppermute(block, "dp", route)


def at(array, index, axis=0):
    return lax.dynamic_index_in_dim(array, index, axis, keepdims=False)


def tied(first, *then):
    return lax.optimization_barrier((first, *then))[1:]


def region(ready, body, *operands):
    blank = lambda *_: jax.tree.map(lambda o: jnp.zeros(o.shape, o.dtype), jax.eval_shape(body, *operands))
    return lax.cond(ready, body, blank, *operands)


class Group:
    def __init__(self, local_pos):
        self.dp, self.mp = lax.axis_size("dp"), lax.axis_size("mp")
        power = local_pos & (local_pos - 1) == 0
        self.size = local_pos if power and self.dp % local_pos == 0 else 1
        self.outer = self.dp // self.size
        self.member = lax.axis_index("dp") % self.size
        self.m = lax.axis_index("mp")
        self.given = self.sent = None
        self.pair = self.mp == 2

    def index(self, r):
        return lax.rem(self.m + r, 2) if self.pair else r

    def swap(self, block):
        return lax.ppermute(block, "mp", [(0, 1), (1, 0)])

    def gather(self, block):
        if self.pair:
            return [block, self.swap(block)]
        every = lax.all_gather(block, "mp", axis=0)
        return [every[r] for r in range(self.mp)]

    def scatter(self, parts, after=None):
        if self.pair:
            got = self.swap(parts[1].astype(BF16))
            if after is not None:
                got = tied(after, got)[0]
            return parts[0].astype(F32) + got.astype(F32)
        return lax.psum_scatter(jnp.stack(parts).astype(F32), "mp", scatter_dimension=0, tiled=False)

    def by_index(self, parts):
        if self.pair:
            first = self.m == 0
            return [jnp.where(first, parts[0], parts[1]), jnp.where(first, parts[1], parts[0])]
        return parts

    def route(self, step):
        return [(i, i ^ step) for i in range(self.dp)]

    def spread(self, blocks, after=None):
        held, bit = blocks[:, None], 1
        while bit < self.size:
            halves = held.reshape((held.shape[0] // 2, 2) + held.shape[1:])
            side = jnp.where((self.member & bit) != 0, 1, 0)
            self.given = at(halves, 1 - side, 1)
            got = lax.ppermute(self.given, "dp", self.route(bit))
            bit *= 2
            if after is not None and bit == self.size:
                got = tied(after, got)[0]
            held = jnp.concatenate([at(halves, side, 1), got], axis=1)
        return held[0]

    def unspread(self, blocks, after=None):
        held, bit = [blocks[s][None] for s in range(self.size)], self.size // 2
        self.sent = jnp.stack(held[bit:])
        while bit:
            got = lax.ppermute(jnp.stack(held[bit:]), "dp", self.route(bit))
            if after is not None:
                got, after = tied(after, got)[0], None
            held = [jnp.concatenate([held[s], got[s]]) for s in range(bit)]
            bit //= 2
        bits = self.size.bit_length() - 1
        turn = [int(format(s, "b").zfill(bits)[::-1] or "0", 2) for s in range(self.size)]
        return self.in_order([held[0][turn[s]] for s in range(self.size)])

    def in_order(self, blocks):
        bit = 1
        while bit < self.size:
            odd = (self.member & bit) != 0
            blocks = [jnp.where(odd, blocks[s ^ bit], blocks[s]) for s in range(self.size)]
            bit *= 2
        return jnp.stack(blocks)

    def sum_scatter(self, values):
        if self.dp & (self.dp - 1):
            return lax.psum_scatter(values, "dp", scatter_dimension=values.ndim - 1, tiled=True)
        me, bit = lax.axis_index("dp"), self.dp // 2
        while bit:
            halves = values.reshape(values.shape[:-1] + (2, values.shape[-1] // 2))
            high = (me & bit) != 0
            keep = jnp.where(high, halves[..., 1, :], halves[..., 0, :])
            give = jnp.where(high, halves[..., 0, :], halves[..., 1, :])
            values = keep + lax.ppermute(give, "dp", self.route(bit))
            bit //= 2
        return values


def params(mib, **more):
    return pltpu.CompilerParams(vmem_limit_bytes=mib * MIB, **more)


def cost(flops, moved, weight):
    return pl.CostEstimate(flops=int(flops * weight), bytes_accessed=int(moved * weight), transcendentals=0)


def call(kernel, grid, args, in_specs, outs, out_specs, scratch, name, flops, prefetch=0, aliases={}, mib=48, weight=WEIGHT):
    moved = sum(a.size * a.dtype.itemsize for a in args) + sum(o.size * o.dtype.itemsize for o in outs)
    return pl.pallas_call(
        kernel,
        grid_spec=pltpu.PrefetchScalarGridSpec(
            num_scalar_prefetch=prefetch,
            grid=grid,
            in_specs=in_specs,
            out_specs=out_specs,
            scratch_shapes=scratch,
        ),
        out_shape=outs,
        input_output_aliases=aliases,
        compiler_params=params(mib),
        cost_estimate=cost(flops, moved, weight),
        name=name,
    )(*args)


def turned(rows, heads):
    return rows.T.reshape(heads, HD, rows.shape[0])


def per_head(scores):
    return scores[:, None, :]


def attention_fwd_kernel(
    heads, held, info, own, other, gain, w_qkv, w_out,
    normed_ref, qkv_ref, probs_ref, context_ref, own_ref, other_ref, keys, values, total
):
    p = pl.program_id(0)
    is_own = (p >= info[0]) & (p < info[0] + held)
    rows = jnp.where(is_own, own[0].astype(F32), other[0].astype(F32))
    scale = lax.rsqrt(jnp.mean(rows * rows, axis=-1, keepdims=True) + EPSILON)
    normed = (rows * scale * gain[0]).astype(BF16)
    normed_ref[0] = normed
    parts = []
    for c in range(3):
        wide = turned(dot(normed, w_qkv[0, c], (1, 0)), heads)
        low = wide.astype(BF16)
        qkv_ref[0, c] = low
        parts.append(low.astype(F32))
    query = parts[0] * 0.125
    keys[p], values[p] = parts[1], parts[2]
    probs_ref[...] = jnp.full(probs_ref.shape, -1e30, F32)

    def score(j, carry):
        probs_ref[0, j] = jnp.sum(query * keys[j], axis=1)
        return carry

    lax.fori_loop(0, p + 1, score, 0)
    scores = probs_ref[0]
    weights = jnp.exp(scores - jnp.max(scores, axis=0, keepdims=True))
    probs_ref[0] = weights / jnp.sum(weights, axis=0, keepdims=True)
    total[...] = jnp.zeros_like(total)

    def mix(j, carry):
        low = probs_ref[0, j].astype(BF16).astype(F32)
        total[...] += per_head(low) * values[j]
        return carry

    lax.fori_loop(0, p + 1, mix, 0)
    context = total[...].reshape(heads * HD, -1).T.astype(BF16)
    context_ref[0] = context
    part = dot(context, w_out[0], (1, 1))

    @pl.when(is_own)
    def _():
        own_ref[0] = part

    @pl.when(jnp.logical_not(is_own))
    def _():
        other_ref[0] = part.astype(BF16)


def attention_fwd(info, own, other, gain, w_qkv, w_out):
    positions, _, width, head_width = w_qkv.shape
    heads = head_width // HD
    held, frames = own.shape[:2]
    rest = other.shape[0]
    block = lambda p, info: jnp.clip(p - info[0], 0, held - 1)
    away = lambda p, info: jnp.clip(p - info[1], 0, rest - 1)
    in_specs = [
        pl.BlockSpec((1, frames, width), lambda p, info: (block(p, info), 0, 0)),
        pl.BlockSpec((1, frames, width), lambda p, info: (away(p, info), 0, 0)),
        pl.BlockSpec((1, 1, width), lambda p, info: (p, 0, 0)),
        pl.BlockSpec((1, 3, width, head_width), lambda p, info: (p, 0, 0, 0)),
        pl.BlockSpec((1, width, head_width), lambda p, info: (p, 0, 0)),
    ]
    outs = [
        jax.ShapeDtypeStruct((positions, frames, width), BF16),
        jax.ShapeDtypeStruct((positions, 3, heads, HD, frames), BF16),
        jax.ShapeDtypeStruct((positions, positions, heads, frames), F32),
        jax.ShapeDtypeStruct((positions, frames, head_width), BF16),
        jax.ShapeDtypeStruct((held, frames, width), F32),
        jax.ShapeDtypeStruct((rest, frames, width), BF16),
    ]
    out_specs = [
        pl.BlockSpec((1, frames, width), lambda p, info: (p, 0, 0)),
        pl.BlockSpec((1, 3, heads, HD, frames), lambda p, info: (p, 0, 0, 0, 0)),
        pl.BlockSpec((1, positions, heads, frames), lambda p, info: (p, 0, 0, 0)),
        pl.BlockSpec((1, frames, head_width), lambda p, info: (p, 0, 0)),
        pl.BlockSpec((1, frames, width), lambda p, info: (block(p, info), 0, 0)),
        pl.BlockSpec((1, frames, width), lambda p, info: (away(p, info), 0, 0)),
    ]
    return call(
        functools.partial(attention_fwd_kernel, heads, held),
        (positions,),
        (info, own, other, gain, w_qkv, w_out),
        in_specs,
        outs,
        out_specs,
        [
            pltpu.VMEM((positions, heads, HD, frames), F32),
            pltpu.VMEM((positions, heads, HD, frames), F32),
            pltpu.VMEM((heads, HD, frames), F32),
        ],
        "attention_fwd",
        8 * positions * frames * width * head_width,
        prefetch=1,
    )


def attention_bwd_kernel(
    positions, heads, held, info, own, other, qkv, probs, w_qkv, w_out,
    d_qkv_ref, own_ref, other_ref, d_keys, d_values, d_query, d_scores
):
    step = pl.program_id(0)
    p = positions - 1 - step

    @pl.when(step == 0)
    def _():
        d_keys[...] = jnp.zeros_like(d_keys)
        d_values[...] = jnp.zeros_like(d_values)

    is_own = (p >= info[0]) & (p < info[0] + held)
    rows = jnp.where(is_own, own[0].astype(F32), other[0].astype(F32)).astype(BF16)
    d_context = dot(rows, w_out[0], (1, 0)).astype(BF16).astype(F32)
    d_context = turned(d_context, heads)
    d_scores[...] = jnp.zeros_like(d_scores)

    def weigh(j, carry):
        d_scores[j] = jnp.sum(d_context * qkv[j, 2].astype(F32), axis=1)
        d_values[j] += per_head(probs[0, j].astype(BF16).astype(F32)) * d_context
        return carry

    lax.fori_loop(0, p + 1, weigh, 0)
    prob, d_probs = probs[0], d_scores[...]
    d_scores[...] = (
        (prob * (d_probs - jnp.sum(prob * d_probs, axis=0, keepdims=True))).astype(BF16).astype(F32)
    ) * 0.125
    d_query[...] = jnp.zeros_like(d_query)
    query = qkv[p, 0].astype(F32)

    def back(j, carry):
        share = per_head(d_scores[j])
        d_query[...] += share * qkv[j, 1].astype(F32)
        d_keys[j] += share * query
        return carry

    lax.fori_loop(0, p + 1, back, 0)
    part = 0.0
    for c, grad in enumerate((d_query[...], d_keys[p], d_values[p])):
        low = grad.reshape(heads * HD, -1).T.astype(BF16)
        d_qkv_ref[0, c] = low
        part = part + dot(low, w_qkv[0, c], (1, 1))

    @pl.when(is_own)
    def _():
        own_ref[0] = part

    @pl.when(jnp.logical_not(is_own))
    def _():
        other_ref[0] = part.astype(BF16)


def attention_bwd(info, own, other, qkv, probs, w_qkv, w_out):
    positions, _, width, head_width = w_qkv.shape
    heads = head_width // HD
    held, frames = own.shape[:2]
    rest = other.shape[0]
    back = lambda s: positions - 1 - s
    block = lambda s, info: jnp.clip(back(s) - info[0], 0, held - 1)
    away = lambda s, info: jnp.clip(back(s) - info[1], 0, rest - 1)
    return call(
        functools.partial(attention_bwd_kernel, positions, heads, held),
        (positions,),
        (info, own, other, qkv, probs, w_qkv, w_out),
        [
            pl.BlockSpec((1, frames, width), lambda s, info: (block(s, info), 0, 0)),
            pl.BlockSpec((1, frames, width), lambda s, info: (away(s, info), 0, 0)),
            pl.BlockSpec((positions, 3, heads, HD, frames), lambda s, info: (0, 0, 0, 0, 0)),
            pl.BlockSpec((1, positions, heads, frames), lambda s, info: (back(s), 0, 0, 0)),
            pl.BlockSpec((1, 3, width, head_width), lambda s, info: (back(s), 0, 0, 0)),
            pl.BlockSpec((1, width, head_width), lambda s, info: (back(s), 0, 0)),
        ],
        [
            jax.ShapeDtypeStruct((positions, 3, frames, head_width), BF16),
            jax.ShapeDtypeStruct((held, frames, width), F32),
            jax.ShapeDtypeStruct((rest, frames, width), BF16),
        ],
        [
            pl.BlockSpec((1, 3, frames, head_width), lambda s, info: (back(s), 0, 0, 0)),
            pl.BlockSpec((1, frames, width), lambda s, info: (block(s, info), 0, 0)),
            pl.BlockSpec((1, frames, width), lambda s, info: (away(s, info), 0, 0)),
        ],
        [
            pltpu.VMEM((positions, heads, HD, frames), F32),
            pltpu.VMEM((positions, heads, HD, frames), F32),
            pltpu.VMEM((heads, HD, frames), F32),
            pltpu.VMEM((positions, heads, frames), F32),
        ],
        "attention_bwd",
        8 * positions * frames * width * head_width,
        prefetch=1,
        mib=56,
    )


def ffn_kernel(info, rows, cot, w_up, w_down, hidden_ref, d_gate_up_ref, d_rows_ref, out_ref):
    gate = dot(rows[...], w_up[0, 0], (1, 0))
    up = dot(rows[...], w_up[0, 1], (1, 0))
    sigma = jax.nn.sigmoid(gate)
    silu = gate * sigma
    hidden = (silu * up).astype(BF16)
    hidden_ref[...] = hidden
    d_hidden = dot(cot[...], w_down[0], (1, 0))
    d_gate = (d_hidden * up * sigma * (1.0 + gate * (1.0 - sigma))).astype(BF16)
    d_up = (d_hidden * silu).astype(BF16)
    d_gate_up_ref[0], d_gate_up_ref[1] = d_gate, d_up
    d_rows = dot(d_gate, w_up[0, 0], (1, 1)) + dot(d_up, w_up[0, 1], (1, 1))
    d_rows_ref[...] = d_rows.astype(d_rows_ref.dtype)
    out_ref[...] = dot(hidden, w_down[0], (1, 1)).astype(out_ref.dtype)


def ffn(position, rows, cot, w_gate_up, w_down, kind):
    count, width = rows.shape
    units = w_down.shape[2]
    block = min(count, 256)
    row = lambda i, info: (i, 0)
    return call(
        ffn_kernel,
        (count // block,),
        (position.reshape(1), rows, cot, w_gate_up, w_down),
        [
            pl.BlockSpec((block, width), row),
            pl.BlockSpec((block, width), row),
            pl.BlockSpec((1, 2, width, units), lambda i, info: (info[0], 0, 0, 0)),
            pl.BlockSpec((1, width, units), lambda i, info: (info[0], 0, 0)),
        ],
        [
            jax.ShapeDtypeStruct((count, units), BF16),
            jax.ShapeDtypeStruct((2, count, units), BF16),
            jax.ShapeDtypeStruct((count, width), kind),
            jax.ShapeDtypeStruct((count, width), kind),
        ],
        [
            pl.BlockSpec((block, units), row),
            pl.BlockSpec((2, block, units), lambda i, info: (0, i, 0)),
            pl.BlockSpec((block, width), row),
            pl.BlockSpec((block, width), row),
        ],
        [],
        "feed_forward",
        12 * count * width * units,
        prefetch=1,
        mib=56,
    )


def weight_grad_kernel(count, *refs):
    lefts, rights, out = refs[:count], refs[count:-1], refs[-1]
    sums = 0.0
    for left, right in zip(lefts, rights, strict=True):
        sums = sums + dot(left[0], right[0, 0], (0, 0))
    out[0, 0, 0] = sums.astype(BF16)


def weight_grad(lefts, rights, outer):
    groups, rows, depth = lefts[0].shape
    parts, width = rights[0].shape[1], rights[0].shape[3]
    block = depth // outer
    if block % LANES:
        full = sum(
            jnp.einsum("grd,gcrn->gcdn", left, right, preferred_element_type=F32)
            for left, right in zip(lefts, rights, strict=True)
        )
        return full.astype(BF16).reshape(groups, parts, outer, block, width).transpose(2, 0, 1, 3, 4)
    count = len(lefts)
    return call(
        functools.partial(weight_grad_kernel, count),
        (groups, parts, outer),
        (*lefts, *rights),
        [pl.BlockSpec((1, rows, block), lambda g, c, o: (g, 0, o))] * count
        + [pl.BlockSpec((1, 1, rows, width), lambda g, c, o: (g, c, 0, 0))] * count,
        [jax.ShapeDtypeStruct((outer, groups, parts, block, width), BF16)],
        [pl.BlockSpec((1, 1, 1, block, width), lambda g, c, o: (o, g, c, 0, 0))],
        [],
        "weight_grad",
        2 * count * groups * parts * rows * depth * width,
    )[0]


def ffn_grad_kernel(count, *refs):
    cots, rows, hidden, d_gate_up = (refs[i * count : (i + 1) * count] for i in range(4))
    out = refs[-1]

    @pl.when(pl.program_id(0) == 0)
    def _():
        out[0, 0] = sum(dot(x[...], y[...], (0, 0)) for x, y in zip(cots, hidden, strict=True)).astype(BF16)

    @pl.when(pl.program_id(0) > 0)
    def _():
        out[0, 0] = sum(dot(x[...], y[0], (0, 0)) for x, y in zip(rows, d_gate_up, strict=True)).astype(BF16)


def ffn_grad(cots, rows, hidden, d_gate_up, outer):
    length, depth = cots[0].shape
    width = hidden[0].shape[1]
    block = depth // outer
    if block % LANES:
        first = sum(dot(x, y, (0, 0)) for x, y in zip(cots, hidden, strict=True))[None]
        others = sum(
            jnp.einsum("rd,crn->cdn", x, y, preferred_element_type=F32)
            for x, y in zip(rows, d_gate_up, strict=True)
        )
        full = jnp.concatenate([first, others]).astype(BF16)
        return full.reshape(3, outer, block, width).transpose(1, 0, 2, 3)
    count = len(cots)
    return call(
        functools.partial(ffn_grad_kernel, count),
        (3, outer),
        (*cots, *rows, *hidden, *d_gate_up),
        [pl.BlockSpec((length, block), lambda c, o: (0, jnp.where(c == 0, o, outer - 1)))] * count
        + [pl.BlockSpec((length, block), lambda c, o: (0, jnp.where(c == 0, 0, o)))] * count
        + [pl.BlockSpec((length, width), lambda c, o: (0, 0))] * count
        + [pl.BlockSpec((1, length, width), lambda c, o: (jnp.maximum(c - 1, 0), 0, 0))] * count,
        [jax.ShapeDtypeStruct((outer, 3, block, width), BF16)],
        [pl.BlockSpec((1, 1, block, width), lambda c, o: (o, c, 0, 0))],
        [],
        "ffn_grad",
        6 * count * length * depth * width,
    )[0]


def norm_back(values, gain, upstream):
    scale = lax.rsqrt(jnp.mean(values * values, axis=-1, keepdims=True) + EPSILON)
    gained = gain[:, None, :] * upstream
    gain_grad = jnp.sum(upstream * values * scale, axis=1)
    value_grad = scale * gained - values * (scale * scale * scale) * jnp.mean(
        gained * values, axis=-1, keepdims=True
    )
    return value_grad, gain_grad


def local(
    frames_in, delays, item_bounds, attn_gain, ffn_gain, w_qkv, w_out, w_gate_up, w_down, cotangent
):
    local_pos, frames, width = frames_in.shape
    positions, head_width = w_qkv.shape[0], w_qkv.shape[3]
    group = Group(local_pos)
    mp, size, outer, pair = group.mp, group.size, group.outer, group.pair
    chunks = 2 if pair and frames % 32 == 0 else 1
    part = frames // chunks

    frame_ids = lax.axis_index("dp") * frames + jnp.arange(frames, dtype=jnp.int32)
    item_start = jnp.where(
        frame_ids >= item_bounds[1],
        item_bounds[1],
        jnp.where(frame_ids >= item_bounds[0], item_bounds[0], 0),
    )

    def delayed(lags, before, block, c):
        padded = jnp.concatenate([before, block], axis=1)
        shifted = jnp.where((lags == 1)[:, None, None], padded[:, 1:-1], padded[:, :-2])
        usable = frame_ids[None, :] - lags[:, None] >= item_start[None, :]
        usable = usable[:, c * part : (c + 1) * part]
        return jnp.where(usable[:, :, None], shifted, jnp.zeros_like(shifted))

    def delayed_chunk(lags, earlier, blocks, c):
        return delayed(lags, blocks[c - 1][:, part - 2 :] if c else earlier, blocks[c], c)

    own_blocks = [frames_in[:, c * part : (c + 1) * part] for c in range(chunks)]
    earlier = shift_frames(frames_in[:, frames - 2 :, :], 1)
    resid = [delayed_chunk(delays, earlier, own_blocks, c) for c in range(chunks)]
    if pair:
        small = jnp.concatenate(
            [attn_gain, jnp.broadcast_to(delays.astype(F32)[:, None], (local_pos, LANES))], axis=1
        )
        small = group.swap(small)
        other_blocks = []
        for block in own_blocks:
            if other_blocks:
                block = tied(other_blocks[-1], block)[0]
            other_blocks.append(group.swap(block))
        other_gain, other_lags = small[:, :width], small[:, width].astype(jnp.int32)
        other_earlier = group.swap(earlier)
        gains = jnp.concatenate(group.by_index([attn_gain, other_gain]))
        first, second = group.m * local_pos, (1 - group.m) * local_pos
        info = jnp.stack([first, second]).astype(jnp.int32)
    else:
        gains = lax.all_gather(attn_gain, "mp", axis=0, tiled=True)
        every = lax.all_gather(resid[0], "mp", axis=0, tiled=True)
        info = jnp.array([0, positions], jnp.int32)
        dummy = jnp.zeros((1, frames, width), BF16)
    gains = gains[:, None, :]

    rows = size * part
    cot_chunks = [cotangent[:, c * part : (c + 1) * part] for c in range(chunks)]
    def by_position(v, after=None):
        blocks = v.reshape((mp, size) + v.shape[1:])
        got = group.spread(jnp.moveaxis(blocks, 1, 0), after)
        got = jnp.moveaxis(got, 0, -3)
        return got.reshape(got.shape[:-3] + (rows, v.shape[-1]))

    normed_all, qkv, probs, context, attn_parts = [], [], [], [], []
    cot_own = [group.spread(chunk).reshape(rows, width) for chunk in cot_chunks]
    step = None
    for c in range(chunks):
        if not pair:
            own, other = every, dummy
        else:
            if c:
                other_blocks[c] = tied(step, other_blocks[c])[0]
            other = delayed_chunk(other_lags, other_earlier, other_blocks, c)
            own, other, cot_own[c] = lax.optimization_barrier((resid[c], other, cot_own[c]))
        *kept, own_part, other_part = attention_fwd(info, own, other, gains, w_qkv, w_out)
        step = own_part
        for held, array in zip((normed_all, qkv, probs, context), kept, strict=True):
            held.append(array)
        attn_parts.append((own_part, other_part))

    lines = [[o * size + k for o in range(outer)] for k in range(size)]

    def sum_lines(part):
        return lax.psum_scatter(
            part, "dp", scatter_dimension=0, axis_index_groups=lines, tiled=True
        )[0]

    middle, ffn_own, given = [], [], None
    for c in range(chunks):
        if pair:
            got = group.swap(attn_parts[c][1])
            if c:
                got = tied(given, got)[0]
            else:
                got, step = lax.optimization_barrier((got, step))
            whole = attn_parts[c][0] + got.astype(F32)
        else:
            whole = lax.psum_scatter(attn_parts[c][0], "mp", scatter_dimension=0, tiled=True)
        middle.append(resid[c].astype(F32) + whole)
        scale = lax.rsqrt(jnp.mean(middle[c] * middle[c], axis=-1, keepdims=True) + EPSILON)
        normed_f = (middle[c] * scale * ffn_gain[:, None, :]).astype(BF16)
        if pair and c == chunks - 1:
            last_normed_f = normed_f
            break
        ffn_own.append(group.spread(normed_f).reshape(rows, width))
        given = group.given
    def feed(r, step, x_rows, g_rows):
        position = jnp.asarray(group.index(r) * size + group.member, jnp.int32)
        kind = F32 if r == 0 or not pair else BF16
        results = []
        for c in range(chunks):
            xs, gs = tied(step, x_rows[c], g_rows[c])
            results.append(ffn(position, xs, gs, w_gate_up, w_down, kind))
            step = results[-1][0]
        return [list(v) for v in zip(*results, strict=True)]

    blocks_of = lambda d_rows: d_rows.astype(BF16).reshape(size, part, width)

    def back_to_positions(d_rows, c, after=None):
        d_normed_f = group.unspread(d_rows, after).astype(F32)
        middle_grad, gain_part = norm_back(middle[c], ffn_gain, d_normed_f)
        return cot_chunks[c].astype(F32) + middle_grad, gain_part

    ffn_sums = []
    if pair:

        def own_positions(x_rows, last, g_rows):
            last = group.spread(last).reshape(rows, width)
            swapped = [group.swap(g_rows[0]), group.swap(x_rows)]
            hidden, d_gate_up, d_own, out_own = feed(0, x_rows, [x_rows, last], g_rows)
            hidden[1], *swapped = lax.optimization_barrier((hidden[1], *swapped))
            grad = ffn_grad(g_rows, [x_rows, last], hidden, d_gate_up, outer)
            return grad, last, swapped, d_own, out_own

        grad_own, last, (cot_other, ffn_other), d_own, out_own = region(
            item_bounds[0] >= 0, own_positions, ffn_own[0], last_normed_f, cot_own
        )
        ffn_sums.append(sum_lines(grad_own))

        def other_positions(x_first, g_first, x_last, g_last, d_own, normed):
            x_rows, g_rows = [x_first, group.swap(x_last)], [g_first, group.swap(g_last)]
            hidden, d_gate_up, d_other, out_other = feed(1, x_first, x_rows, g_rows)
            normed = [by_position(v) for v in normed]
            got = group.swap(d_other[0])
            got, *normed = lax.optimization_barrier((got, *normed))
            d_first = blocks_of(d_own[0] + got.astype(F32))
            hidden[0] = tied(d_first, hidden[0])[0]
            grad = ffn_grad(g_rows, x_rows, hidden, d_gate_up, outer)
            d_middle, gain_part = back_to_positions(d_first, 0, grad)
            got = tied(grad, group.swap(d_other[1]))[0]
            d_late, gain_late = back_to_positions(blocks_of(d_own[1] + got.astype(F32)), 1)
            low = d_middle.astype(BF16)
            d_middle = [d_middle, d_late]
            lows = [low, d_late.astype(BF16)]
            return grad, d_middle, lows, group.swap(low), gain_part + gain_late, out_other, normed

        grad, d_middle, d_middle_low, d_first, ffn_gain_part, out_other, normed_rows = region(
            item_bounds[0] >= 0,
            other_positions,
            ffn_other,
            cot_other,
            last,
            cot_own[1],
            d_own,
            normed_all,
        )
        out_parts = [out_own, out_other]
        ffn_sums[0], d_middle_low[1] = lax.optimization_barrier((ffn_sums[0], d_middle_low[1]))
        ffn_sums.append(sum_lines(tied(ffn_sums[0], grad)[0]))
    else:
        normed_rows = [by_position(normed_all[0])]
        context_rows = [by_position(context[0])[:, None]]
        cot_rows = [[block] for block in group.gather(cot_own[0])]
        ffn_rows = [[block] for block in group.gather(ffn_own[0])]
        d_parts, out_parts = [], []
        for r in range(mp):
            hidden, d_gate_up, d_part, out_part = feed(r, step, ffn_rows[r], cot_rows[r])
            d_parts.append(d_part[0])
            out_parts.append(out_part)
            step = ffn_grad(cot_rows[r], ffn_rows[r], hidden, d_gate_up, outer)
            ffn_sums.append(sum_lines(step))
        d_mid, ffn_gain_part = back_to_positions(blocks_of(group.scatter(d_parts)), 0)
        d_middle, d_middle_low = [d_mid], [d_mid.astype(BF16)]
        d_middle_all = [lax.all_gather(d_middle_low[0], "mp", axis=0, tiled=True)]
        d_middle_two = [[d_middle_all[0], dummy]]

    def finish(whole):
        depth, n = whole.shape[-2:]
        blocks = whole.reshape(whole.shape[:-2] + (size, depth // size, n))
        return group.in_order(group.spread(jnp.moveaxis(blocks, -3, 0)))

    def ends(d_normed_a, out_rows, middle, d_middle, ffn_gain_part):
        mixed = []
        for c in range(chunks):
            got = group.unspread(blocks_of(out_rows[c]))
            mixed.append((middle[c] + got.astype(F32)).astype(BF16))
        mixed = jnp.concatenate(mixed, axis=1)

        d_resid, attn_gain_part = [], 0.0
        for c in range(chunks):
            resid_grad, gain_part = norm_back(resid[c].astype(F32), attn_gain, d_normed_a[c])
            attn_gain_part = attn_gain_part + gain_part
            d_resid.append(d_middle[c] + resid_grad)
        d_resid = jnp.concatenate(d_resid, axis=1)
        usable = frame_ids[None, :] - delays[:, None] >= item_start[None, :]
        spread = jnp.where(usable[:, :, None], d_resid, 0.0)
        one = (delays == 1)[:, None, None]
        blank = jnp.zeros((local_pos, 1, width), F32)
        head = spread[:, :2]
        placed = jnp.where(one, jnp.concatenate([blank, head[:, :1]], axis=1), head)
        returned = shift_frames(placed, -1)
        tail = jnp.concatenate([spread, blank, blank], axis=1)
        input_grad = jnp.where(one, tail[:, 1 : frames + 1], tail[:, 2:])
        input_grad = input_grad + jnp.pad(returned, ((0, 0), (frames - 2, 0), (0, 0)))
        gains = group.sum_scatter(jnp.stack([attn_gain_part, ffn_gain_part]))
        return mixed, input_grad, gains[0], gains[1]

    if pair:

        def attention_back(d_middle_low, d_first, qkv, probs, normed_rows, out_other, sums):
            d_last = group.swap(d_middle_low[1])
            two = [[d_middle_low[0], d_first], [d_middle_low[1], d_last]]
            d_qkv, own_first, other_first = attention_bwd(info, *two[0], qkv[0], probs[0], w_qkv, w_out)
            two[1] = tied(d_qkv, *two[1])
            sums = finish(sums)
            *two[1], sums = lax.optimization_barrier((*two[1], sums))
            d_later, own_last, other_last = attention_bwd(info, *two[1], qkv[1], probs[1], w_qkv, w_out)
            d_qkv, d_later = by_position(d_qkv), by_position(d_later)
            sent = [group.swap(block) for block in out_other]
            d_later, *sent = lax.optimization_barrier((d_later, *sent))
            qkv_part = weight_grad(normed_rows, [d_qkv, d_later], outer)
            return qkv_part, d_last, [own_first, own_last], [other_first, other_last], sent, sums

        qkv_part, d_last, own_parts, other_parts, sent, ffn_first = region(
            item_bounds[0] >= 0,
            attention_back,
            d_middle_low,
            d_first,
            qkv,
            probs,
            normed_rows,
            out_parts[1],
            ffn_sums[0],
        )
        ffn_sums[1], own_parts[0] = lax.optimization_barrier((ffn_sums[1], own_parts[0]))
        qkv_sums = sum_lines(tied(ffn_sums[1], qkv_part)[0])

        def others(d_two, context, own_parts, other_parts, out_own, sent, middle, d_middle, sums, gain_part):
            d_normed_a = [group.scatter([own_parts[c], other_parts[c]]) for c in range(chunks)]
            out_rows = [out_own[c] + sent[c].astype(F32) for c in range(chunks)]
            held = [by_position(v)[:, None] for v in context]
            out_part = weight_grad(
                [by_position(jnp.concatenate(group.by_index(two))) for two in d_two], held, outer
            )
            return out_part, finish(sums), *ends(d_normed_a, out_rows, middle, d_middle, gain_part)

        out_part, ffn_last, mixed, input_grad, attn_gain_grad, ffn_gain_grad = region(
            item_bounds[0] >= 0,
            others,
            [[d_middle_low[0], d_first], [d_middle_low[1], d_last]],
            context,
            own_parts,
            other_parts,
            out_parts[0],
            sent,
            middle,
            d_middle,
            ffn_sums[1],
            ffn_gain_part,
        )
        qkv_sums, out_part = lax.optimization_barrier((qkv_sums, out_part))
        out_sums = sum_lines(out_part)
        ffn_done = [ffn_first, ffn_last]
    else:
        d_qkv, own_part, _ = attention_bwd(info, *d_middle_two[0], qkv[0], probs[0], w_qkv, w_out)
        d_normed_a = [lax.psum_scatter(own_part, "mp", scatter_dimension=0, tiled=True)]
        out_part = weight_grad([by_position(d_middle_all[0])], context_rows, outer)
        qkv_part = weight_grad(normed_rows, [by_position(d_qkv)], outer)
        out_rows = [group.scatter([out_parts[r][0] for r in range(mp)])]
        qkv_sums, out_sums = sum_lines(qkv_part), sum_lines(out_part)
        ffn_done = [finish(sums) for sums in ffn_sums]
        mixed, input_grad, attn_gain_grad, ffn_gain_grad = ends(
            d_normed_a, out_rows, middle, d_middle, ffn_gain_part
        )

    qkv_done = finish(qkv_sums)
    out_done = finish(tied(qkv_done, out_sums)[0])
    ffn_done = jnp.stack(group.by_index(ffn_done)).astype(F32)
    ffn_done = ffn_done.reshape((positions,) + ffn_done.shape[2:])
    down_grad, gate_up_grad = ffn_done[:, 0], ffn_done[:, 1:]

    def both(got):
        got = jnp.swapaxes(got, 0, 1)
        return got.reshape((positions,) + got.shape[2:]).astype(F32)

    out_grad, qkv_grad = both(out_done)[:, 0], both(qkv_done)
    return (
        mixed,
        input_grad,
        attn_gain_grad,
        ffn_gain_grad,
        qkv_grad,
        out_grad,
        gate_up_grad,
        down_grad,
    )


def solution(mesh):
    placed = (
        P("mp", "dp", None),
        P("mp"),
        P(),
        P("mp", None),
        P("mp", None),
        P(None, None, None, "mp"),
        P(None, None, "mp"),
        P(None, None, None, "mp"),
        P(None, None, "mp"),
        P("mp", "dp", None),
    )
    return jax.shard_map(
        local,
        mesh=mesh,
        in_specs=placed,
        out_specs=(
            P("mp", "dp", None),
            P("mp", "dp", None),
            P("mp", "dp"),
            P("mp", "dp"),
            P(None, None, "dp", "mp"),
            P(None, "dp", "mp"),
            P(None, None, "dp", "mp"),
            P(None, "dp", "mp"),
        ),
        check_vma=False,
    )
```

```python
import functools

import jax
import jax.numpy as jnp
from jax import lax
from jax.experimental import pallas as pl
from jax.experimental.pallas import tpu as pltpu
from jax.sharding import PartitionSpec as P

HD = 64
LANES = 128
EPSILON = 1e-05
BF16 = jnp.bfloat16
F32 = jnp.float32
MIB = 1024 * 1024
WEIGHT = 100


def dot(left, right, contract):
    return lax.dot_general(left, right, ((contract[:1], contract[1:]), ((), ())), preferred_element_type=F32)


def shift_frames(block, distance):
    devices = range(lax.axis_size("dp"))
    route = [(i - distance, i) for i in devices if i - distance in devices]
    return lax.ppermute(block, "dp", route)


def at(array, index, axis=0):
    return lax.dynamic_index_in_dim(array, index, axis, keepdims=False)


def tied(first, *then):
    return lax.optimization_barrier((first, *then))[1:]


def region(ready, body, *operands):
    blank = lambda *_: jax.tree.map(lambda o: jnp.zeros(o.shape, o.dtype), jax.eval_shape(body, *operands))
    return lax.cond(ready, body, blank, *operands)


class Group:
    def __init__(self, local_pos):
        self.dp, self.mp = lax.axis_size("dp"), lax.axis_size("mp")
        power = local_pos & (local_pos - 1) == 0
        self.size = local_pos if power and self.dp % local_pos == 0 else 1
        self.outer = self.dp // self.size
        self.member = lax.axis_index("dp") % self.size
        self.m = lax.axis_index("mp")
        self.pair = self.mp == 2

    def index(self, r):
        return lax.rem(self.m + r, 2) if self.pair else r

    def swap(self, block):
        return lax.ppermute(block, "mp", [(0, 1), (1, 0)])

    def gather(self, block):
        if self.pair:
            return [block, self.swap(block)]
        every = lax.all_gather(block, "mp", axis=0)
        return [every[r] for r in range(self.mp)]

    def scatter(self, parts, after=None):
        if self.pair:
            got = self.swap(parts[1].astype(BF16))
            if after is not None:
                got = tied(after, got)[0]
            return parts[0].astype(F32) + got.astype(F32)
        return lax.psum_scatter(jnp.stack(parts).astype(F32), "mp", scatter_dimension=0, tiled=False)

    def by_index(self, parts):
        if self.pair:
            first = self.m == 0
            return [jnp.where(first, parts[0], parts[1]), jnp.where(first, parts[1], parts[0])]
        return parts

    def route(self, step):
        return [(i, i ^ step) for i in range(self.dp)]

    def begin(self, blocks):
        held, bit = blocks[:, None], 1
        while bit < self.size:
            halves = held.reshape((held.shape[0] // 2, 2) + held.shape[1:])
            side = jnp.where((self.member & bit) != 0, 1, 0)
            keep, give = at(halves, side, 1), at(halves, 1 - side, 1)
            if 2 * bit == self.size:
                return keep, give
            held = jnp.concatenate([keep, lax.ppermute(give, "dp", self.route(bit))], axis=1)
            bit *= 2
        return held, None

    def end(self, keep, give):
        if give is None:
            return keep[0]
        return jnp.concatenate([keep, lax.ppermute(give, "dp", self.route(self.size // 2))], axis=1)[0]

    def spread(self, blocks):
        return self.end(*self.begin(blocks))

    def begin_back(self, blocks):
        held, half = [blocks[s][None] for s in range(self.size)], self.size // 2
        return held, jnp.stack(held[half:]) if half else None

    def first_back(self, give):
        return give if give is None else lax.ppermute(give, "dp", self.route(self.size // 2))

    def end_back(self, held, got):
        bit = self.size // 2
        while bit:
            if got is None:
                got = lax.ppermute(jnp.stack(held[bit:]), "dp", self.route(bit))
            held, got = [jnp.concatenate([held[s], got[s]]) for s in range(bit)], None
            bit //= 2
        bits = self.size.bit_length() - 1
        turn = [int(format(s, "b").zfill(bits)[::-1] or "0", 2) for s in range(self.size)]
        return self.in_order([held[0][turn[s]] for s in range(self.size)])

    def unspread(self, blocks):
        held, give = self.begin_back(blocks)
        return self.end_back(held, self.first_back(give))

    def in_order(self, blocks):
        bit = 1
        while bit < self.size:
            odd = (self.member & bit) != 0
            blocks = [jnp.where(odd, blocks[s ^ bit], blocks[s]) for s in range(self.size)]
            bit *= 2
        return jnp.stack(blocks)

    def sum_scatter(self, values):
        if self.dp & (self.dp - 1):
            return lax.psum_scatter(values, "dp", scatter_dimension=values.ndim - 1, tiled=True)
        me, bit = lax.axis_index("dp"), self.dp // 2
        while bit:
            halves = values.reshape(values.shape[:-1] + (2, values.shape[-1] // 2))
            high = (me & bit) != 0
            keep = jnp.where(high, halves[..., 1, :], halves[..., 0, :])
            give = jnp.where(high, halves[..., 0, :], halves[..., 1, :])
            values = keep + lax.ppermute(give, "dp", self.route(bit))
            bit //= 2
        return values


def params(mib, **more):
    return pltpu.CompilerParams(vmem_limit_bytes=mib * MIB, **more)


def cost(flops, moved, weight):
    return pl.CostEstimate(flops=int(flops * weight), bytes_accessed=int(moved * weight), transcendentals=0)


def call(kernel, grid, args, in_specs, outs, out_specs, scratch, name, flops, prefetch=0, aliases={}, mib=48, weight=WEIGHT):
    moved = sum(a.size * a.dtype.itemsize for a in args) + sum(o.size * o.dtype.itemsize for o in outs)
    return pl.pallas_call(
        kernel,
        grid_spec=pltpu.PrefetchScalarGridSpec(
            num_scalar_prefetch=prefetch,
            grid=grid,
            in_specs=in_specs,
            out_specs=out_specs,
            scratch_shapes=scratch,
        ),
        out_shape=outs,
        input_output_aliases=aliases,
        compiler_params=params(mib),
        cost_estimate=cost(flops, moved, weight),
        name=name,
    )(*args)


def turned(rows, heads):
    return rows.T.reshape(heads, HD, rows.shape[0])


def per_head(scores):
    return scores[:, None, :]


def attention_fwd_kernel(
    heads, held, info, own, other, gain, w_qkv, w_out,
    normed_ref, qkv_ref, probs_ref, context_ref, own_ref, other_ref, keys, values, total
):
    p = pl.program_id(0)
    is_own = (p >= info[0]) & (p < info[0] + held)
    rows = jnp.where(is_own, own[0].astype(F32), other[0].astype(F32))
    scale = lax.rsqrt(jnp.mean(rows * rows, axis=-1, keepdims=True) + EPSILON)
    normed = (rows * scale * gain[0]).astype(BF16)
    normed_ref[0] = normed
    parts = []
    for c in range(3):
        low = turned(dot(normed, w_qkv[0, c], (1, 0)).astype(BF16), heads)
        qkv_ref[0, c] = low
        parts.append(low.astype(F32))
    query = parts[0] * 0.125
    keys[p], values[p] = parts[1], parts[2]
    probs_ref[...] = jnp.full(probs_ref.shape, -1e30, F32)

    def score(j, carry):
        probs_ref[0, j] = jnp.sum(query * keys[j], axis=1)
        return carry

    lax.fori_loop(0, p + 1, score, 0)
    scores = probs_ref[0]
    weights = jnp.exp(scores - jnp.max(scores, axis=0, keepdims=True))
    probs_ref[0] = weights / jnp.sum(weights, axis=0, keepdims=True)
    total[...] = jnp.zeros_like(total)

    def mix(j, carry):
        low = probs_ref[0, j].astype(BF16).astype(F32)
        total[...] += per_head(low) * values[j]
        return carry

    lax.fori_loop(0, p + 1, mix, 0)
    context = total[...].astype(BF16).reshape(heads * HD, -1).T
    context_ref[0] = context
    part = dot(context, w_out[0], (1, 1))

    @pl.when(is_own)
    def _():
        own_ref[0] = part

    @pl.when(jnp.logical_not(is_own))
    def _():
        other_ref[0] = part.astype(BF16)


def attention_fwd(info, own, other, gain, w_qkv, w_out):
    positions, _, width, head_width = w_qkv.shape
    heads = head_width // HD
    held, frames = own.shape[:2]
    rest = other.shape[0]
    block = lambda p, info: jnp.clip(p - info[0], 0, held - 1)
    away = lambda p, info: jnp.clip(p - info[1], 0, rest - 1)
    in_specs = [
        pl.BlockSpec((1, frames, width), lambda p, info: (block(p, info), 0, 0)),
        pl.BlockSpec((1, frames, width), lambda p, info: (away(p, info), 0, 0)),
        pl.BlockSpec((1, 1, width), lambda p, info: (p, 0, 0)),
        pl.BlockSpec((1, 3, width, head_width), lambda p, info: (p, 0, 0, 0)),
        pl.BlockSpec((1, width, head_width), lambda p, info: (p, 0, 0)),
    ]
    outs = [
        jax.ShapeDtypeStruct((positions, frames, width), BF16),
        jax.ShapeDtypeStruct((positions, 3, heads, HD, frames), BF16),
        jax.ShapeDtypeStruct((positions, positions, heads, frames), F32),
        jax.ShapeDtypeStruct((positions, frames, head_width), BF16),
        jax.ShapeDtypeStruct((held, frames, width), F32),
        jax.ShapeDtypeStruct((rest, frames, width), BF16),
    ]
    out_specs = [
        pl.BlockSpec((1, frames, width), lambda p, info: (p, 0, 0)),
        pl.BlockSpec((1, 3, heads, HD, frames), lambda p, info: (p, 0, 0, 0, 0)),
        pl.BlockSpec((1, positions, heads, frames), lambda p, info: (p, 0, 0, 0)),
        pl.BlockSpec((1, frames, head_width), lambda p, info: (p, 0, 0)),
        pl.BlockSpec((1, frames, width), lambda p, info: (block(p, info), 0, 0)),
        pl.BlockSpec((1, frames, width), lambda p, info: (away(p, info), 0, 0)),
    ]
    return call(
        functools.partial(attention_fwd_kernel, heads, held),
        (positions,),
        (info, own, other, gain, w_qkv, w_out),
        in_specs,
        outs,
        out_specs,
        [
            pltpu.VMEM((positions, heads, HD, frames), F32),
            pltpu.VMEM((positions, heads, HD, frames), F32),
            pltpu.VMEM((heads, HD, frames), F32),
        ],
        "attention_fwd",
        8 * positions * frames * width * head_width,
        prefetch=1,
    )


def attention_bwd_kernel(
    positions, heads, held, info, own, other, qkv, probs, w_qkv, w_out,
    d_qkv_ref, own_ref, other_ref, d_keys, d_values, d_query, d_scores
):
    step = pl.program_id(0)
    p = positions - 1 - step

    @pl.when(step == 0)
    def _():
        d_keys[...] = jnp.zeros_like(d_keys)
        d_values[...] = jnp.zeros_like(d_values)

    is_own = (p >= info[0]) & (p < info[0] + held)
    rows = jnp.where(is_own, own[0].astype(F32), other[0].astype(F32)).astype(BF16)
    d_context = turned(dot(rows, w_out[0], (1, 0)).astype(BF16), heads).astype(F32)
    d_scores[...] = jnp.zeros_like(d_scores)

    def weigh(j, carry):
        d_scores[j] = jnp.sum(d_context * qkv[j, 2].astype(F32), axis=1)
        d_values[j] += per_head(probs[0, j].astype(BF16).astype(F32)) * d_context
        return carry

    lax.fori_loop(0, p + 1, weigh, 0)
    prob, d_probs = probs[0], d_scores[...]
    d_scores[...] = (
        (prob * (d_probs - jnp.sum(prob * d_probs, axis=0, keepdims=True))).astype(BF16).astype(F32)
    ) * 0.125
    d_query[...] = jnp.zeros_like(d_query)
    query = qkv[p, 0].astype(F32)

    def back(j, carry):
        share = per_head(d_scores[j])
        d_query[...] += share * qkv[j, 1].astype(F32)
        d_keys[j] += share * query
        return carry

    lax.fori_loop(0, p + 1, back, 0)
    part = 0.0
    for c, grad in enumerate((d_query[...], d_keys[p], d_values[p])):
        low = grad.astype(BF16).reshape(heads * HD, -1).T
        d_qkv_ref[0, c] = low
        part = part + dot(low, w_qkv[0, c], (1, 1))

    @pl.when(is_own)
    def _():
        own_ref[0] = part

    @pl.when(jnp.logical_not(is_own))
    def _():
        other_ref[0] = part.astype(BF16)


def attention_bwd(info, own, other, qkv, probs, w_qkv, w_out):
    positions, _, width, head_width = w_qkv.shape
    heads = head_width // HD
    held, frames = own.shape[:2]
    rest = other.shape[0]
    back = lambda s: positions - 1 - s
    block = lambda s, info: jnp.clip(back(s) - info[0], 0, held - 1)
    away = lambda s, info: jnp.clip(back(s) - info[1], 0, rest - 1)
    return call(
        functools.partial(attention_bwd_kernel, positions, heads, held),
        (positions,),
        (info, own, other, qkv, probs, w_qkv, w_out),
        [
            pl.BlockSpec((1, frames, width), lambda s, info: (block(s, info), 0, 0)),
            pl.BlockSpec((1, frames, width), lambda s, info: (away(s, info), 0, 0)),
            pl.BlockSpec((positions, 3, heads, HD, frames), lambda s, info: (0, 0, 0, 0, 0)),
            pl.BlockSpec((1, positions, heads, frames), lambda s, info: (back(s), 0, 0, 0)),
            pl.BlockSpec((1, 3, width, head_width), lambda s, info: (back(s), 0, 0, 0)),
            pl.BlockSpec((1, width, head_width), lambda s, info: (back(s), 0, 0)),
        ],
        [
            jax.ShapeDtypeStruct((positions, 3, frames, head_width), BF16),
            jax.ShapeDtypeStruct((held, frames, width), F32),
            jax.ShapeDtypeStruct((rest, frames, width), BF16),
        ],
        [
            pl.BlockSpec((1, 3, frames, head_width), lambda s, info: (back(s), 0, 0, 0)),
            pl.BlockSpec((1, frames, width), lambda s, info: (block(s, info), 0, 0)),
            pl.BlockSpec((1, frames, width), lambda s, info: (away(s, info), 0, 0)),
        ],
        [
            pltpu.VMEM((positions, heads, HD, frames), F32),
            pltpu.VMEM((positions, heads, HD, frames), F32),
            pltpu.VMEM((heads, HD, frames), F32),
            pltpu.VMEM((positions, heads, frames), F32),
        ],
        "attention_bwd",
        8 * positions * frames * width * head_width,
        prefetch=1,
        mib=56,
    )


def ffn_kernel(info, rows, cot, w_up, w_down, hidden_ref, d_gate_up_ref, d_rows_ref, out_ref):
    gate = dot(rows[...], w_up[0, 0], (1, 0))
    up = dot(rows[...], w_up[0, 1], (1, 0))
    sigma = jax.nn.sigmoid(gate)
    silu = gate * sigma
    hidden = (silu * up).astype(BF16)
    hidden_ref[...] = hidden
    d_hidden = dot(cot[...], w_down[0], (1, 0))
    d_gate = (d_hidden * up * sigma * (1.0 + gate * (1.0 - sigma))).astype(BF16)
    d_up = (d_hidden * silu).astype(BF16)
    d_gate_up_ref[0], d_gate_up_ref[1] = d_gate, d_up
    d_rows = dot(d_gate, w_up[0, 0], (1, 1)) + dot(d_up, w_up[0, 1], (1, 1))
    d_rows_ref[...] = d_rows.astype(d_rows_ref.dtype)
    out_ref[...] = dot(hidden, w_down[0], (1, 1)).astype(out_ref.dtype)


def ffn(position, rows, cot, w_gate_up, w_down, kind):
    count, width = rows.shape
    units = w_down.shape[2]
    block = min(count, 256)
    row = lambda i, info: (i, 0)
    return call(
        ffn_kernel,
        (count // block,),
        (position.reshape(1), rows, cot, w_gate_up, w_down),
        [
            pl.BlockSpec((block, width), row),
            pl.BlockSpec((block, width), row),
            pl.BlockSpec((1, 2, width, units), lambda i, info: (info[0], 0, 0, 0)),
            pl.BlockSpec((1, width, units), lambda i, info: (info[0], 0, 0)),
        ],
        [
            jax.ShapeDtypeStruct((count, units), BF16),
            jax.ShapeDtypeStruct((2, count, units), BF16),
            jax.ShapeDtypeStruct((count, width), kind),
            jax.ShapeDtypeStruct((count, width), kind),
        ],
        [
            pl.BlockSpec((block, units), row),
            pl.BlockSpec((2, block, units), lambda i, info: (0, i, 0)),
            pl.BlockSpec((block, width), row),
            pl.BlockSpec((block, width), row),
        ],
        [],
        "feed_forward",
        12 * count * width * units,
        prefetch=1,
        mib=56,
    )


def weight_grad_kernel(count, *refs):
    lefts, rights, out = refs[:count], refs[count:-1], refs[-1]
    sums = 0.0
    for left, right in zip(lefts, rights, strict=True):
        sums = sums + dot(left[0], right[0, 0], (0, 0))
    out[0, 0, 0] = sums.astype(BF16)


def weight_grad(lefts, rights, outer):
    groups, rows, depth = lefts[0].shape
    parts, width = rights[0].shape[1], rights[0].shape[3]
    block = depth // outer
    if block % LANES:
        full = sum(
            jnp.einsum("grd,gcrn->gcdn", left, right, preferred_element_type=F32)
            for left, right in zip(lefts, rights, strict=True)
        )
        return full.astype(BF16).reshape(groups, parts, outer, block, width).transpose(2, 0, 1, 3, 4)
    count = len(lefts)
    return call(
        functools.partial(weight_grad_kernel, count),
        (groups, parts, outer),
        (*lefts, *rights),
        [pl.BlockSpec((1, rows, block), lambda g, c, o: (g, 0, o))] * count
        + [pl.BlockSpec((1, 1, rows, width), lambda g, c, o: (g, c, 0, 0))] * count,
        [jax.ShapeDtypeStruct((outer, groups, parts, block, width), BF16)],
        [pl.BlockSpec((1, 1, 1, block, width), lambda g, c, o: (o, g, c, 0, 0))],
        [],
        "weight_grad",
        2 * count * groups * parts * rows * depth * width,
    )[0]


def ffn_grad_kernel(count, *refs):
    cots, rows, hidden, d_gate_up = (refs[i * count : (i + 1) * count] for i in range(4))
    out = refs[-1]

    @pl.when(pl.program_id(0) == 0)
    def _():
        out[0, 0] = sum(dot(x[...], y[...], (0, 0)) for x, y in zip(cots, hidden, strict=True)).astype(BF16)

    @pl.when(pl.program_id(0) > 0)
    def _():
        out[0, 0] = sum(dot(x[...], y[0], (0, 0)) for x, y in zip(rows, d_gate_up, strict=True)).astype(BF16)


def ffn_grad(cots, rows, hidden, d_gate_up, outer):
    length, depth = cots[0].shape
    width = hidden[0].shape[1]
    block = depth // outer
    if block % LANES:
        first = sum(dot(x, y, (0, 0)) for x, y in zip(cots, hidden, strict=True))[None]
        others = sum(
            jnp.einsum("rd,crn->cdn", x, y, preferred_element_type=F32)
            for x, y in zip(rows, d_gate_up, strict=True)
        )
        full = jnp.concatenate([first, others]).astype(BF16)
        return full.reshape(3, outer, block, width).transpose(1, 0, 2, 3)
    count = len(cots)
    return call(
        functools.partial(ffn_grad_kernel, count),
        (3, outer),
        (*cots, *rows, *hidden, *d_gate_up),
        [pl.BlockSpec((length, block), lambda c, o: (0, jnp.where(c == 0, o, outer - 1)))] * count
        + [pl.BlockSpec((length, block), lambda c, o: (0, jnp.where(c == 0, 0, o)))] * count
        + [pl.BlockSpec((length, width), lambda c, o: (0, 0))] * count
        + [pl.BlockSpec((1, length, width), lambda c, o: (jnp.maximum(c - 1, 0), 0, 0))] * count,
        [jax.ShapeDtypeStruct((outer, 3, block, width), BF16)],
        [pl.BlockSpec((1, 1, block, width), lambda c, o: (o, c, 0, 0))],
        [],
        "ffn_grad",
        6 * count * length * depth * width,
    )[0]


def norm_back(values, gain, upstream):
    scale = lax.rsqrt(jnp.mean(values * values, axis=-1, keepdims=True) + EPSILON)
    gained = gain[:, None, :] * upstream
    gain_grad = jnp.sum(upstream * values * scale, axis=1)
    value_grad = scale * gained - values * (scale * scale * scale) * jnp.mean(
        gained * values, axis=-1, keepdims=True
    )
    return value_grad, gain_grad


def local(
    frames_in, delays, item_bounds, attn_gain, ffn_gain, w_qkv, w_out, w_gate_up, w_down, cotangent
):
    local_pos, frames, width = frames_in.shape
    positions, head_width = w_qkv.shape[0], w_qkv.shape[3]
    group = Group(local_pos)
    mp, size, outer, pair = group.mp, group.size, group.outer, group.pair
    chunks = 2 if pair and frames % 32 == 0 else 1
    part = frames // chunks

    frame_ids = lax.axis_index("dp") * frames + jnp.arange(frames, dtype=jnp.int32)
    item_start = jnp.where(
        frame_ids >= item_bounds[1],
        item_bounds[1],
        jnp.where(frame_ids >= item_bounds[0], item_bounds[0], 0),
    )

    def delayed(lags, before, block, c):
        padded = jnp.concatenate([before, block], axis=1)
        shifted = jnp.where((lags == 1)[:, None, None], padded[:, 1:-1], padded[:, :-2])
        usable = frame_ids[None, :] - lags[:, None] >= item_start[None, :]
        usable = usable[:, c * part : (c + 1) * part]
        return jnp.where(usable[:, :, None], shifted, jnp.zeros_like(shifted))

    def delayed_chunk(lags, earlier, blocks, c):
        return delayed(lags, blocks[c - 1][:, part - 2 :] if c else earlier, blocks[c], c)

    own_blocks = [frames_in[:, c * part : (c + 1) * part] for c in range(chunks)]
    rows = size * part
    *own_blocks, late_cotangent = lax.optimization_barrier((*own_blocks, cotangent))
    cot_chunks = [late_cotangent[:, c * part : (c + 1) * part] for c in range(chunks)]
    earlier = shift_frames(frames_in[:, frames - 2 :, :], 1)
    resid = [delayed_chunk(delays, earlier, own_blocks, c) for c in range(chunks)]
    if pair:
        small = jnp.concatenate(
            [attn_gain, jnp.broadcast_to(delays.astype(F32)[:, None], (local_pos, LANES))], axis=1
        )
        small = group.swap(small)
        other_blocks = []
        for block in own_blocks:
            if other_blocks:
                block = tied(other_blocks[-1], block)[0]
            other_blocks.append(group.swap(block))
        other_gain, other_lags = small[:, :width], small[:, width].astype(jnp.int32)
        other_earlier = group.swap(earlier)
        gains = jnp.concatenate(group.by_index([attn_gain, other_gain]))
        first, second = group.m * local_pos, (1 - group.m) * local_pos
        info = jnp.stack([first, second]).astype(jnp.int32)
    else:
        gains = lax.all_gather(attn_gain, "mp", axis=0, tiled=True)
        every = lax.all_gather(resid[0], "mp", axis=0, tiled=True)
        info = jnp.array([0, positions], jnp.int32)
        dummy = jnp.zeros((1, frames, width), BF16)
    gains = gains[:, None, :]

    def begin_position(v):
        return group.begin(jnp.moveaxis(v.reshape((mp, size) + v.shape[1:]), 1, 0))

    def end_position(keep, give):
        got = jnp.moveaxis(group.end(keep, give), 0, -3)
        return got.reshape(got.shape[:-3] + (rows, got.shape[-1]))

    def by_position(v):
        return end_position(*begin_position(v))

    normed_all, qkv, probs, context, attn_parts = [], [], [], [], []
    cot_own = [group.spread(chunk).reshape(rows, width) for chunk in cot_chunks]
    step = None
    for c in range(chunks):
        if not pair:
            own, other = every, dummy
        else:
            if c:
                other_blocks[c] = tied(step, other_blocks[c])[0]
            other = delayed_chunk(other_lags, other_earlier, other_blocks, c)
            own, other, cot_own[c] = lax.optimization_barrier((resid[c], other, cot_own[c]))
        *kept, own_part, other_part = attention_fwd(info, own, other, gains, w_qkv, w_out)
        step = own_part
        for held, array in zip((normed_all, qkv, probs, context), kept, strict=True):
            held.append(array)
        attn_parts.append((own_part, other_part))

    lines = [[o * size + k for o in range(outer)] for k in range(size)]

    def sum_lines(part):
        return lax.psum_scatter(
            part, "dp", scatter_dimension=0, axis_index_groups=lines, tiled=True
        )[0]

    middle, ffn_own, given = [], [], None
    for c in range(chunks):
        if pair:
            got = group.swap(attn_parts[c][1])
            if c:
                got = tied(given, got)[0]
            else:
                got, step = lax.optimization_barrier((got, step))
            whole = attn_parts[c][0] + got.astype(F32)
        else:
            whole = lax.psum_scatter(attn_parts[c][0], "mp", scatter_dimension=0, tiled=True)
        middle.append(resid[c].astype(F32) + whole)
        scale = lax.rsqrt(jnp.mean(middle[c] * middle[c], axis=-1, keepdims=True) + EPSILON)
        normed_f = (middle[c] * scale * ffn_gain[:, None, :]).astype(BF16)
        if pair and c == chunks - 1:
            last_normed_f = normed_f
            break
        keep, given = group.begin(normed_f)
        ffn_own.append(group.end(keep, given).reshape(rows, width))
    def feed(r, step, x_rows, g_rows, beside=()):
        position = jnp.asarray(group.index(r) * size + group.member, jnp.int32)
        kind = F32 if r == 0 or not pair else BF16
        results, moved = [], []
        for c in range(chunks):
            xs, gs = tied(step, x_rows[c], g_rows[c])
            if beside:
                keep, give = begin_position(beside[c])
                xs, give = lax.optimization_barrier((xs, give))
                moved.append(end_position(keep, give))
            result = ffn(position, xs, gs, w_gate_up, w_down, kind)
            step = result[0]
            if beside:
                step, moved[c] = lax.optimization_barrier((step, moved[c]))
                result = (step, *result[1:])
            results.append(result)
        return [list(v) for v in zip(*results, strict=True)], moved

    blocks_of = lambda d_rows: d_rows.astype(BF16).reshape(size, part, width)

    def back_to_positions(d_normed_f, c):
        middle_grad, gain_part = norm_back(middle[c], ffn_gain, d_normed_f.astype(F32))
        return cot_chunks[c].astype(F32) + middle_grad, gain_part

    ffn_sums = []
    if pair:

        def own_positions(x_rows, last, g_rows):
            last = group.spread(last).reshape(rows, width)
            swapped = [group.swap(g_rows[0]), group.swap(x_rows)]
            (hidden, d_gate_up, d_own, out_own), _ = feed(0, x_rows, [x_rows, last], g_rows)
            hidden[1], *swapped = lax.optimization_barrier((hidden[1], *swapped))
            grad = ffn_grad(g_rows, [x_rows, last], hidden, d_gate_up, outer)
            return grad, last, swapped, d_own, out_own

        grad_own, last, (cot_other, ffn_other), d_own, out_own = region(
            item_bounds[0] >= 0, own_positions, ffn_own[0], last_normed_f, cot_own
        )
        ffn_sums.append(sum_lines(grad_own))

        def other_positions(x_first, g_first, x_last, g_last, d_own, normed, held):
            x_rows, g_rows = [x_first, group.swap(x_last)], [g_first, group.swap(g_last)]
            (hidden, d_gate_up, d_other, out_other), normed = feed(1, x_first, x_rows, g_rows, normed)
            got = [group.swap(block) for block in d_other]
            hidden[1], got[0] = lax.optimization_barrier((hidden[1], got[0]))
            keep, give = group.begin_back(blocks_of(d_own[0] + got[0].astype(F32)))
            hidden[0], give = lax.optimization_barrier((hidden[0], give))
            grad = ffn_grad(g_rows, x_rows, hidden, d_gate_up, outer)
            moved = group.first_back(give)
            grad, moved, got[1] = lax.optimization_barrier((grad, moved, got[1]))
            d_middle, gain_part = back_to_positions(group.end_back(keep, moved), 0)
            d_last = group.unspread(blocks_of(d_own[1] + got[1].astype(F32)))
            d_late, gain_late = back_to_positions(d_last, 1)
            held = [by_position(v)[:, None] for v in held]
            low = d_middle.astype(BF16)
            d_middle = [d_middle, d_late]
            lows = [low, d_late.astype(BF16)]
            return grad, d_middle, lows, group.swap(low), gain_part + gain_late, out_other, normed, held

        grad, d_middle, d_middle_low, d_first, ffn_gain_part, out_other, normed_rows, context_rows = region(
            item_bounds[0] >= 0,
            other_positions,
            ffn_other,
            cot_other,
            last,
            cot_own[1],
            d_own,
            normed_all,
            context,
        )
        out_parts = [out_own, out_other]
        ffn_sums[0], d_middle_low[1] = lax.optimization_barrier((ffn_sums[0], d_middle_low[1]))
        ffn_sums.append(sum_lines(tied(ffn_sums[0], grad)[0]))
    else:
        normed_rows = [by_position(normed_all[0])]
        context_rows = [by_position(context[0])[:, None]]
        cot_rows = [[block] for block in group.gather(cot_own[0])]
        ffn_rows = [[block] for block in group.gather(ffn_own[0])]
        d_parts, out_parts = [], []
        for r in range(mp):
            (hidden, d_gate_up, d_part, out_part), _ = feed(r, step, ffn_rows[r], cot_rows[r])
            d_parts.append(d_part[0])
            out_parts.append(out_part)
            step = ffn_grad(cot_rows[r], ffn_rows[r], hidden, d_gate_up, outer)
            ffn_sums.append(sum_lines(step))
        d_mid, ffn_gain_part = back_to_positions(group.unspread(blocks_of(group.scatter(d_parts))), 0)
        d_middle, d_middle_low = [d_mid], [d_mid.astype(BF16)]
        d_middle_all = [lax.all_gather(d_middle_low[0], "mp", axis=0, tiled=True)]
        d_middle_two = [[d_middle_all[0], dummy]]

    def finish(whole):
        depth, n = whole.shape[-2:]
        blocks = whole.reshape(whole.shape[:-2] + (size, depth // size, n))
        return group.in_order(group.spread(jnp.moveaxis(blocks, -3, 0)))

    def ffn_grads(sums):
        done = jnp.stack(group.by_index([finish(v) for v in sums])).astype(F32)
        done = done.reshape((positions,) + done.shape[2:])
        return done[:, 0], done[:, 1:]

    def ends(d_normed_a, out_rows, middle, d_middle, ffn_gain_part):
        mixed = []
        for c in range(chunks):
            got = group.unspread(blocks_of(out_rows[c]))
            mixed.append((middle[c] + got.astype(F32)).astype(BF16))
        mixed = jnp.concatenate(mixed, axis=1)

        d_resid, attn_gain_part = [], 0.0
        for c in range(chunks):
            resid_grad, gain_part = norm_back(resid[c].astype(F32), attn_gain, d_normed_a[c])
            attn_gain_part = attn_gain_part + gain_part
            d_resid.append(d_middle[c] + resid_grad)
        d_resid = jnp.concatenate(d_resid, axis=1)
        usable = frame_ids[None, :] - delays[:, None] >= item_start[None, :]
        spread = jnp.where(usable[:, :, None], d_resid, 0.0)
        one = (delays == 1)[:, None, None]
        blank = jnp.zeros((local_pos, 1, width), F32)
        head = spread[:, :2]
        placed = jnp.where(one, jnp.concatenate([blank, head[:, :1]], axis=1), head)
        returned = shift_frames(placed, -1)
        tail = jnp.concatenate([spread, blank, blank], axis=1)
        input_grad = jnp.where(one, tail[:, 1 : frames + 1], tail[:, 2:])
        input_grad = input_grad + jnp.pad(returned, ((0, 0), (frames - 2, 0), (0, 0)))
        gains = group.sum_scatter(jnp.stack([attn_gain_part, ffn_gain_part]))
        return mixed, input_grad, gains[0], gains[1]

    if pair:

        def attention_back(d_middle_low, d_first, qkv, probs, normed_rows, context_rows, out_other):
            d_last = group.swap(d_middle_low[1])
            two = [[d_middle_low[0], d_first], [d_middle_low[1], d_last]]
            keep, give = begin_position(jnp.concatenate(group.by_index(two[0])))
            *two[0], give = lax.optimization_barrier((*two[0], give))
            mid_first = end_position(keep, give)
            d_qkv, own_first, other_first = attention_bwd(info, *two[0], qkv[0], probs[0], w_qkv, w_out)
            d_qkv, mid_first, two[1][1] = lax.optimization_barrier((d_qkv, mid_first, two[1][1]))
            keep, give = begin_position(d_qkv)
            *two[1], give = lax.optimization_barrier((*two[1], give))
            d_later, own_last, other_last = attention_bwd(info, *two[1], qkv[1], probs[1], w_qkv, w_out)
            d_qkv = end_position(keep, give)
            sent = [group.swap(block) for block in out_other]
            d_later, d_qkv, sent[0] = lax.optimization_barrier((d_later, d_qkv, sent[0]))
            d_later = by_position(d_later)
            keep, give = begin_position(jnp.concatenate(group.by_index(two[1])))
            d_later, give = lax.optimization_barrier((d_later, give))
            mid_last = end_position(keep, give)
            qkv_part = weight_grad(normed_rows, [d_qkv, d_later], outer)
            qkv_part, mid_last, sent[1] = lax.optimization_barrier((qkv_part, mid_last, sent[1]))
            out_part = weight_grad([mid_first, mid_last], context_rows, outer)
            return qkv_part, out_part, [own_first, own_last], [other_first, other_last], sent

        qkv_part, out_part, own_parts, other_parts, sent = region(
            item_bounds[0] >= 0,
            attention_back,
            d_middle_low,
            d_first,
            qkv,
            probs,
            normed_rows,
            context_rows,
            out_parts[1],
        )
        ffn_sums[1], own_parts[0] = lax.optimization_barrier((ffn_sums[1], own_parts[0]))
        qkv_part, out_part = tied(ffn_sums[1], qkv_part, out_part)
        qkv_sums, out_sums = sum_lines(qkv_part), sum_lines(out_part)

        def others(own_parts, other_parts, out_own, sent, middle, d_middle, sums, gain_part):
            d_normed_a = [group.scatter([own_parts[c], other_parts[c]]) for c in range(chunks)]
            out_rows = [out_own[c] + sent[c].astype(F32) for c in range(chunks)]
            return ffn_grads(sums), *ends(d_normed_a, out_rows, middle, d_middle, gain_part)

        (down_grad, gate_up_grad), mixed, input_grad, attn_gain_grad, ffn_gain_grad = region(
            item_bounds[0] >= 0,
            others,
            own_parts,
            other_parts,
            out_parts[0],
            sent,
            middle,
            d_middle,
            ffn_sums,
            ffn_gain_part,
        )
        qkv_sums, out_sums, attn_gain_grad = lax.optimization_barrier((qkv_sums, out_sums, attn_gain_grad))
    else:
        d_qkv, own_part, _ = attention_bwd(info, *d_middle_two[0], qkv[0], probs[0], w_qkv, w_out)
        d_normed_a = [lax.psum_scatter(own_part, "mp", scatter_dimension=0, tiled=True)]
        out_part = weight_grad([by_position(d_middle_all[0])], context_rows, outer)
        qkv_part = weight_grad(normed_rows, [by_position(d_qkv)], outer)
        out_rows = [group.scatter([out_parts[r][0] for r in range(mp)])]
        qkv_sums, out_sums = sum_lines(qkv_part), sum_lines(out_part)
        down_grad, gate_up_grad = ffn_grads(ffn_sums)
        mixed, input_grad, attn_gain_grad, ffn_gain_grad = ends(
            d_normed_a, out_rows, middle, d_middle, ffn_gain_part
        )

    qkv_done = finish(qkv_sums)
    out_done = finish(tied(qkv_done, out_sums)[0])
    def both(got):
        got = jnp.swapaxes(got, 0, 1)
        return got.reshape((positions,) + got.shape[2:]).astype(F32)

    out_grad, qkv_grad = both(out_done)[:, 0], both(qkv_done)
    return (
        mixed,
        input_grad,
        attn_gain_grad,
        ffn_gain_grad,
        qkv_grad,
        out_grad,
        gate_up_grad,
        down_grad,
    )


def solution(mesh):
    placed = (
        P("mp", "dp", None),
        P("mp"),
        P(),
        P("mp", None),
        P("mp", None),
        P(None, None, None, "mp"),
        P(None, None, "mp"),
        P(None, None, None, "mp"),
        P(None, None, "mp"),
        P("mp", "dp", None),
    )
    return jax.shard_map(
        local,
        mesh=mesh,
        in_specs=placed,
        out_specs=(
            P("mp", "dp", None),
            P("mp", "dp", None),
            P("mp", "dp"),
            P("mp", "dp"),
            P(None, None, "dp", "mp"),
            P(None, "dp", "mp"),
            P(None, None, "dp", "mp"),
            P(None, "dp", "mp"),
        ),
        check_vma=False,
    )
```

```python
import functools

import jax
import jax.numpy as jnp
from jax import lax
from jax.experimental import pallas as pl
from jax.experimental.pallas import tpu as pltpu
from jax.sharding import PartitionSpec as P

HD = 64
LANES = 128
EPSILON = 1e-05
BF16 = jnp.bfloat16
F32 = jnp.float32
MIB = 1024 * 1024
WEIGHT = 100


def dot(left, right, contract):
    return lax.dot_general(left, right, ((contract[:1], contract[1:]), ((), ())), preferred_element_type=F32)


def shift_frames(block, distance):
    devices = range(lax.axis_size("dp"))
    route = [(i - distance, i) for i in devices if i - distance in devices]
    return lax.ppermute(block, "dp", route)


def at(array, index, axis=0):
    return lax.dynamic_index_in_dim(array, index, axis, keepdims=False)


def tied(first, *then):
    return lax.optimization_barrier((first, *then))[1:]


def region(ready, body, *operands):
    blank = lambda *_: jax.tree.map(lambda o: jnp.zeros(o.shape, o.dtype), jax.eval_shape(body, *operands))
    return lax.cond(ready, body, blank, *operands)


class Group:
    def __init__(self, local_pos):
        self.dp, self.mp = lax.axis_size("dp"), lax.axis_size("mp")
        power = local_pos & (local_pos - 1) == 0
        self.size = local_pos if power and self.dp % local_pos == 0 else 1
        self.outer = self.dp // self.size
        self.member = lax.axis_index("dp") % self.size
        self.m = lax.axis_index("mp")
        self.pair = self.mp == 2

    def index(self, r):
        return lax.rem(self.m + r, 2) if self.pair else r

    def swap(self, block):
        return lax.ppermute(block, "mp", [(0, 1), (1, 0)])

    def gather(self, block):
        if self.pair:
            return [block, self.swap(block)]
        every = lax.all_gather(block, "mp", axis=0)
        return [every[r] for r in range(self.mp)]

    def scatter(self, parts, after=None):
        if self.pair:
            got = self.swap(parts[1].astype(BF16))
            if after is not None:
                got = tied(after, got)[0]
            return parts[0].astype(F32) + got.astype(F32)
        return lax.psum_scatter(jnp.stack(parts).astype(F32), "mp", scatter_dimension=0, tiled=False)

    def by_index(self, parts):
        if self.pair:
            first = self.m == 0
            return [jnp.where(first, parts[0], parts[1]), jnp.where(first, parts[1], parts[0])]
        return parts

    def route(self, step):
        return [(i, i ^ step) for i in range(self.dp)]

    def begin(self, blocks):
        held, bit = blocks[:, None], 1
        while bit < self.size:
            halves = held.reshape((held.shape[0] // 2, 2) + held.shape[1:])
            side = jnp.where((self.member & bit) != 0, 1, 0)
            keep, give = at(halves, side, 1), at(halves, 1 - side, 1)
            if 2 * bit == self.size:
                return keep, give
            held = jnp.concatenate([keep, lax.ppermute(give, "dp", self.route(bit))], axis=1)
            bit *= 2
        return held, None

    def end(self, keep, give):
        if give is None:
            return keep[0]
        return jnp.concatenate([keep, lax.ppermute(give, "dp", self.route(self.size // 2))], axis=1)[0]

    def spread(self, blocks):
        return self.end(*self.begin(blocks))

    def begin_back(self, blocks):
        held, half = [blocks[s][None] for s in range(self.size)], self.size // 2
        return held, jnp.stack(held[half:]) if half else None

    def first_back(self, give):
        return give if give is None else lax.ppermute(give, "dp", self.route(self.size // 2))

    def end_back(self, held, got):
        bit = self.size // 2
        while bit:
            if got is None:
                got = lax.ppermute(jnp.stack(held[bit:]), "dp", self.route(bit))
            held, got = [jnp.concatenate([held[s], got[s]]) for s in range(bit)], None
            bit //= 2
        bits = self.size.bit_length() - 1
        turn = [int(format(s, "b").zfill(bits)[::-1] or "0", 2) for s in range(self.size)]
        return self.in_order([held[0][turn[s]] for s in range(self.size)])

    def unspread(self, blocks):
        held, give = self.begin_back(blocks)
        return self.end_back(held, self.first_back(give))

    def in_order(self, blocks):
        bit = 1
        while bit < self.size:
            odd = (self.member & bit) != 0
            blocks = [jnp.where(odd, blocks[s ^ bit], blocks[s]) for s in range(self.size)]
            bit *= 2
        return jnp.stack(blocks)

    def sum_scatter(self, values):
        if self.dp & (self.dp - 1):
            return lax.psum_scatter(values, "dp", scatter_dimension=values.ndim - 1, tiled=True)
        me, bit = lax.axis_index("dp"), self.dp // 2
        while bit:
            halves = values.reshape(values.shape[:-1] + (2, values.shape[-1] // 2))
            high = (me & bit) != 0
            keep = jnp.where(high, halves[..., 1, :], halves[..., 0, :])
            give = jnp.where(high, halves[..., 0, :], halves[..., 1, :])
            values = keep + lax.ppermute(give, "dp", self.route(bit))
            bit //= 2
        return values


def params(mib, **more):
    return pltpu.CompilerParams(vmem_limit_bytes=mib * MIB, **more)


def cost(flops, moved, weight):
    return pl.CostEstimate(flops=int(flops * weight), bytes_accessed=int(moved * weight), transcendentals=0)


def call(kernel, grid, args, in_specs, outs, out_specs, scratch, name, flops, prefetch=0, aliases={}, mib=48, weight=WEIGHT):
    moved = sum(a.size * a.dtype.itemsize for a in args) + sum(o.size * o.dtype.itemsize for o in outs)
    return pl.pallas_call(
        kernel,
        grid_spec=pltpu.PrefetchScalarGridSpec(
            num_scalar_prefetch=prefetch,
            grid=grid,
            in_specs=in_specs,
            out_specs=out_specs,
            scratch_shapes=scratch,
        ),
        out_shape=outs,
        input_output_aliases=aliases,
        compiler_params=params(mib),
        cost_estimate=cost(flops, moved, weight),
        name=name,
    )(*args)


def turned(rows, heads):
    return rows.T.reshape(heads, HD, rows.shape[0])


def per_head(scores):
    return scores[:, None, :]


def attention_fwd_kernel(
    heads, held, info, own, other, gain, w_qkv, w_out,
    normed_ref, qkv_ref, probs_ref, context_ref, own_ref, other_ref, keys, values, total
):
    p = pl.program_id(0)
    is_own = (p >= info[0]) & (p < info[0] + held)
    rows = jnp.where(is_own, own[0].astype(F32), other[0].astype(F32))
    scale = lax.rsqrt(jnp.mean(rows * rows, axis=-1, keepdims=True) + EPSILON)
    normed = (rows * scale * gain[0]).astype(BF16)
    normed_ref[0] = normed
    parts = []
    for c in range(3):
        low = turned(dot(normed, w_qkv[0, c], (1, 0)).astype(BF16), heads)
        qkv_ref[0, c] = low
        parts.append(low.astype(F32))
    query = parts[0] * 0.125
    keys[p], values[p] = parts[1], parts[2]
    probs_ref[...] = jnp.full(probs_ref.shape, -1e30, F32)

    def score(j, carry):
        probs_ref[0, j] = jnp.sum(query * keys[j], axis=1)
        return carry

    lax.fori_loop(0, p + 1, score, 0)
    scores = probs_ref[0]
    weights = jnp.exp(scores - jnp.max(scores, axis=0, keepdims=True))
    probs_ref[0] = weights / jnp.sum(weights, axis=0, keepdims=True)
    total[...] = jnp.zeros_like(total)

    def mix(j, carry):
        low = probs_ref[0, j].astype(BF16).astype(F32)
        total[...] += per_head(low) * values[j]
        return carry

    lax.fori_loop(0, p + 1, mix, 0)
    context = total[...].astype(BF16).reshape(heads * HD, -1).T
    context_ref[0] = context
    part = dot(context, w_out[0], (1, 1))

    @pl.when(is_own)
    def _():
        own_ref[0] = part

    @pl.when(jnp.logical_not(is_own))
    def _():
        other_ref[0] = part.astype(BF16)


def attention_fwd(info, own, other, gain, w_qkv, w_out):
    positions, _, width, head_width = w_qkv.shape
    heads = head_width // HD
    held, frames = own.shape[:2]
    rest = other.shape[0]
    block = lambda p, info: jnp.clip(p - info[0], 0, held - 1)
    away = lambda p, info: jnp.clip(p - info[1], 0, rest - 1)
    in_specs = [
        pl.BlockSpec((1, frames, width), lambda p, info: (block(p, info), 0, 0)),
        pl.BlockSpec((1, frames, width), lambda p, info: (away(p, info), 0, 0)),
        pl.BlockSpec((1, 1, width), lambda p, info: (p, 0, 0)),
        pl.BlockSpec((1, 3, width, head_width), lambda p, info: (p, 0, 0, 0)),
        pl.BlockSpec((1, width, head_width), lambda p, info: (p, 0, 0)),
    ]
    outs = [
        jax.ShapeDtypeStruct((positions, frames, width), BF16),
        jax.ShapeDtypeStruct((positions, 3, heads, HD, frames), BF16),
        jax.ShapeDtypeStruct((positions, positions, heads, frames), F32),
        jax.ShapeDtypeStruct((positions, frames, head_width), BF16),
        jax.ShapeDtypeStruct((held, frames, width), F32),
        jax.ShapeDtypeStruct((rest, frames, width), BF16),
    ]
    out_specs = [
        pl.BlockSpec((1, frames, width), lambda p, info: (p, 0, 0)),
        pl.BlockSpec((1, 3, heads, HD, frames), lambda p, info: (p, 0, 0, 0, 0)),
        pl.BlockSpec((1, positions, heads, frames), lambda p, info: (p, 0, 0, 0)),
        pl.BlockSpec((1, frames, head_width), lambda p, info: (p, 0, 0)),
        pl.BlockSpec((1, frames, width), lambda p, info: (block(p, info), 0, 0)),
        pl.BlockSpec((1, frames, width), lambda p, info: (away(p, info), 0, 0)),
    ]
    return call(
        functools.partial(attention_fwd_kernel, heads, held),
        (positions,),
        (info, own, other, gain, w_qkv, w_out),
        in_specs,
        outs,
        out_specs,
        [
            pltpu.VMEM((positions, heads, HD, frames), F32),
            pltpu.VMEM((positions, heads, HD, frames), F32),
            pltpu.VMEM((heads, HD, frames), F32),
        ],
        "attention_fwd",
        8 * positions * frames * width * head_width,
        prefetch=1,
    )


def attention_bwd_kernel(
    positions, heads, held, info, own, other, qkv, probs, w_qkv, w_out,
    d_qkv_ref, own_ref, other_ref, d_keys, d_values, d_query, d_scores
):
    step = pl.program_id(0)
    p = positions - 1 - step

    @pl.when(step == 0)
    def _():
        d_keys[...] = jnp.zeros_like(d_keys)
        d_values[...] = jnp.zeros_like(d_values)

    is_own = (p >= info[0]) & (p < info[0] + held)
    rows = jnp.where(is_own, own[0].astype(F32), other[0].astype(F32)).astype(BF16)
    d_context = turned(dot(rows, w_out[0], (1, 0)).astype(BF16), heads).astype(F32)
    d_scores[...] = jnp.zeros_like(d_scores)

    def weigh(j, carry):
        d_scores[j] = jnp.sum(d_context * qkv[j, 2].astype(F32), axis=1)
        d_values[j] += per_head(probs[0, j].astype(BF16).astype(F32)) * d_context
        return carry

    lax.fori_loop(0, p + 1, weigh, 0)
    prob, d_probs = probs[0], d_scores[...]
    d_scores[...] = (
        (prob * (d_probs - jnp.sum(prob * d_probs, axis=0, keepdims=True))).astype(BF16).astype(F32)
    ) * 0.125
    d_query[...] = jnp.zeros_like(d_query)
    query = qkv[p, 0].astype(F32)

    def back(j, carry):
        share = per_head(d_scores[j])
        d_query[...] += share * qkv[j, 1].astype(F32)
        d_keys[j] += share * query
        return carry

    lax.fori_loop(0, p + 1, back, 0)
    part = 0.0
    for c, grad in enumerate((d_query[...], d_keys[p], d_values[p])):
        low = grad.astype(BF16).reshape(heads * HD, -1).T
        d_qkv_ref[0, c] = low
        part = part + dot(low, w_qkv[0, c], (1, 1))

    @pl.when(is_own)
    def _():
        own_ref[0] = part

    @pl.when(jnp.logical_not(is_own))
    def _():
        other_ref[0] = part.astype(BF16)


def attention_bwd(info, own, other, qkv, probs, w_qkv, w_out):
    positions, _, width, head_width = w_qkv.shape
    heads = head_width // HD
    held, frames = own.shape[:2]
    rest = other.shape[0]
    back = lambda s: positions - 1 - s
    block = lambda s, info: jnp.clip(back(s) - info[0], 0, held - 1)
    away = lambda s, info: jnp.clip(back(s) - info[1], 0, rest - 1)
    return call(
        functools.partial(attention_bwd_kernel, positions, heads, held),
        (positions,),
        (info, own, other, qkv, probs, w_qkv, w_out),
        [
            pl.BlockSpec((1, frames, width), lambda s, info: (block(s, info), 0, 0)),
            pl.BlockSpec((1, frames, width), lambda s, info: (away(s, info), 0, 0)),
            pl.BlockSpec((positions, 3, heads, HD, frames), lambda s, info: (0, 0, 0, 0, 0)),
            pl.BlockSpec((1, positions, heads, frames), lambda s, info: (back(s), 0, 0, 0)),
            pl.BlockSpec((1, 3, width, head_width), lambda s, info: (back(s), 0, 0, 0)),
            pl.BlockSpec((1, width, head_width), lambda s, info: (back(s), 0, 0)),
        ],
        [
            jax.ShapeDtypeStruct((positions, 3, frames, head_width), BF16),
            jax.ShapeDtypeStruct((held, frames, width), F32),
            jax.ShapeDtypeStruct((rest, frames, width), BF16),
        ],
        [
            pl.BlockSpec((1, 3, frames, head_width), lambda s, info: (back(s), 0, 0, 0)),
            pl.BlockSpec((1, frames, width), lambda s, info: (block(s, info), 0, 0)),
            pl.BlockSpec((1, frames, width), lambda s, info: (away(s, info), 0, 0)),
        ],
        [
            pltpu.VMEM((positions, heads, HD, frames), F32),
            pltpu.VMEM((positions, heads, HD, frames), F32),
            pltpu.VMEM((heads, HD, frames), F32),
            pltpu.VMEM((positions, heads, frames), F32),
        ],
        "attention_bwd",
        8 * positions * frames * width * head_width,
        prefetch=1,
        mib=56,
    )


def ffn_kernel(info, rows, cot, w_up, w_down, hidden_ref, d_gate_up_ref, d_rows_ref, out_ref):
    gate = dot(rows[...], w_up[0, 0], (1, 0))
    up = dot(rows[...], w_up[0, 1], (1, 0))
    sigma = jax.nn.sigmoid(gate)
    silu = gate * sigma
    hidden = (silu * up).astype(BF16)
    hidden_ref[...] = hidden
    d_hidden = dot(cot[...], w_down[0], (1, 0))
    d_gate = (d_hidden * up * sigma * (1.0 + gate * (1.0 - sigma))).astype(BF16)
    d_up = (d_hidden * silu).astype(BF16)
    d_gate_up_ref[0], d_gate_up_ref[1] = d_gate, d_up
    d_rows = dot(d_gate, w_up[0, 0], (1, 1)) + dot(d_up, w_up[0, 1], (1, 1))
    d_rows_ref[...] = d_rows.astype(d_rows_ref.dtype)
    out_ref[...] = dot(hidden, w_down[0], (1, 1)).astype(out_ref.dtype)


def ffn(position, rows, cot, w_gate_up, w_down, kind):
    count, width = rows.shape
    units = w_down.shape[2]
    block = min(count, 256)
    row = lambda i, info: (i, 0)
    return call(
        ffn_kernel,
        (count // block,),
        (position.reshape(1), rows, cot, w_gate_up, w_down),
        [
            pl.BlockSpec((block, width), row),
            pl.BlockSpec((block, width), row),
            pl.BlockSpec((1, 2, width, units), lambda i, info: (info[0], 0, 0, 0)),
            pl.BlockSpec((1, width, units), lambda i, info: (info[0], 0, 0)),
        ],
        [
            jax.ShapeDtypeStruct((count, units), BF16),
            jax.ShapeDtypeStruct((2, count, units), BF16),
            jax.ShapeDtypeStruct((count, width), kind),
            jax.ShapeDtypeStruct((count, width), kind),
        ],
        [
            pl.BlockSpec((block, units), row),
            pl.BlockSpec((2, block, units), lambda i, info: (0, i, 0)),
            pl.BlockSpec((block, width), row),
            pl.BlockSpec((block, width), row),
        ],
        [],
        "feed_forward",
        12 * count * width * units,
        prefetch=1,
        mib=56,
    )


def weight_grad_kernel(count, *refs):
    lefts, rights, out = refs[:count], refs[count:-1], refs[-1]
    sums = 0.0
    for left, right in zip(lefts, rights, strict=True):
        sums = sums + dot(left[0], right[0, 0], (0, 0))
    out[0, 0, 0] = sums.astype(BF16)


def weight_grad(lefts, rights, outer):
    groups, rows, depth = lefts[0].shape
    parts, width = rights[0].shape[1], rights[0].shape[3]
    block = depth // outer
    if block % LANES:
        full = sum(
            jnp.einsum("grd,gcrn->gcdn", left, right, preferred_element_type=F32)
            for left, right in zip(lefts, rights, strict=True)
        )
        return full.astype(BF16).reshape(groups, parts, outer, block, width).transpose(2, 0, 1, 3, 4)
    count = len(lefts)
    return call(
        functools.partial(weight_grad_kernel, count),
        (groups, parts, outer),
        (*lefts, *rights),
        [pl.BlockSpec((1, rows, block), lambda g, c, o: (g, 0, o))] * count
        + [pl.BlockSpec((1, 1, rows, width), lambda g, c, o: (g, c, 0, 0))] * count,
        [jax.ShapeDtypeStruct((outer, groups, parts, block, width), BF16)],
        [pl.BlockSpec((1, 1, 1, block, width), lambda g, c, o: (o, g, c, 0, 0))],
        [],
        "weight_grad",
        2 * count * groups * parts * rows * depth * width,
    )[0]


def ffn_grad_kernel(count, *refs):
    cots, rows, hidden, d_gate_up = (refs[i * count : (i + 1) * count] for i in range(4))
    out = refs[-1]

    @pl.when(pl.program_id(0) == 0)
    def _():
        out[0, 0] = sum(dot(x[...], y[...], (0, 0)) for x, y in zip(cots, hidden, strict=True)).astype(BF16)

    @pl.when(pl.program_id(0) > 0)
    def _():
        out[0, 0] = sum(dot(x[...], y[0], (0, 0)) for x, y in zip(rows, d_gate_up, strict=True)).astype(BF16)


def ffn_grad(cots, rows, hidden, d_gate_up, outer):
    length, depth = cots[0].shape
    width = hidden[0].shape[1]
    block = depth // outer
    if block % LANES:
        first = sum(dot(x, y, (0, 0)) for x, y in zip(cots, hidden, strict=True))[None]
        others = sum(
            jnp.einsum("rd,crn->cdn", x, y, preferred_element_type=F32)
            for x, y in zip(rows, d_gate_up, strict=True)
        )
        full = jnp.concatenate([first, others]).astype(BF16)
        return full.reshape(3, outer, block, width).transpose(1, 0, 2, 3)
    count = len(cots)
    return call(
        functools.partial(ffn_grad_kernel, count),
        (3, outer),
        (*cots, *rows, *hidden, *d_gate_up),
        [pl.BlockSpec((length, block), lambda c, o: (0, jnp.where(c == 0, o, outer - 1)))] * count
        + [pl.BlockSpec((length, block), lambda c, o: (0, jnp.where(c == 0, 0, o)))] * count
        + [pl.BlockSpec((length, width), lambda c, o: (0, 0))] * count
        + [pl.BlockSpec((1, length, width), lambda c, o: (jnp.maximum(c - 1, 0), 0, 0))] * count,
        [jax.ShapeDtypeStruct((outer, 3, block, width), BF16)],
        [pl.BlockSpec((1, 1, block, width), lambda c, o: (o, c, 0, 0))],
        [],
        "ffn_grad",
        6 * count * length * depth * width,
    )[0]


def norm_back(values, gain, upstream):
    scale = lax.rsqrt(jnp.mean(values * values, axis=-1, keepdims=True) + EPSILON)
    gained = gain[:, None, :] * upstream
    gain_grad = jnp.sum(upstream * values * scale, axis=1)
    value_grad = scale * gained - values * (scale * scale * scale) * jnp.mean(
        gained * values, axis=-1, keepdims=True
    )
    return value_grad, gain_grad


def local(
    frames_in, delays, item_bounds, attn_gain, ffn_gain, w_qkv, w_out, w_gate_up, w_down, cotangent
):
    local_pos, frames, width = frames_in.shape
    positions, head_width = w_qkv.shape[0], w_qkv.shape[3]
    group = Group(local_pos)
    mp, size, outer, pair = group.mp, group.size, group.outer, group.pair
    chunks = 2 if pair and frames % 32 == 0 else 1
    part = frames // chunks

    frame_ids = lax.axis_index("dp") * frames + jnp.arange(frames, dtype=jnp.int32)
    item_start = jnp.where(
        frame_ids >= item_bounds[1],
        item_bounds[1],
        jnp.where(frame_ids >= item_bounds[0], item_bounds[0], 0),
    )

    def delayed(lags, before, block, c):
        padded = jnp.concatenate([before, block], axis=1)
        shifted = jnp.where((lags == 1)[:, None, None], padded[:, 1:-1], padded[:, :-2])
        usable = frame_ids[None, :] - lags[:, None] >= item_start[None, :]
        usable = usable[:, c * part : (c + 1) * part]
        return jnp.where(usable[:, :, None], shifted, jnp.zeros_like(shifted))

    def delayed_chunk(lags, earlier, blocks, c):
        return delayed(lags, blocks[c - 1][:, part - 2 :] if c else earlier, blocks[c], c)

    own_blocks = [frames_in[:, c * part : (c + 1) * part] for c in range(chunks)]
    rows = size * part
    *own_blocks, late_cotangent = lax.optimization_barrier((*own_blocks, cotangent))
    cot_chunks = [late_cotangent[:, c * part : (c + 1) * part] for c in range(chunks)]
    earlier = shift_frames(frames_in[:, frames - 2 :, :], 1)
    resid = [delayed_chunk(delays, earlier, own_blocks, c) for c in range(chunks)]
    if pair:
        small = jnp.concatenate(
            [attn_gain, jnp.broadcast_to(delays.astype(F32)[:, None], (local_pos, LANES))], axis=1
        )
        small = group.swap(small)
        other_blocks = []
        for block in own_blocks:
            if other_blocks:
                block = tied(other_blocks[-1], block)[0]
            other_blocks.append(group.swap(block))
        other_gain, other_lags = small[:, :width], small[:, width].astype(jnp.int32)
        other_earlier = group.swap(earlier)
        gains = jnp.concatenate(group.by_index([attn_gain, other_gain]))
        first, second = group.m * local_pos, (1 - group.m) * local_pos
        info = jnp.stack([first, second]).astype(jnp.int32)
    else:
        gains = lax.all_gather(attn_gain, "mp", axis=0, tiled=True)
        every = lax.all_gather(resid[0], "mp", axis=0, tiled=True)
        info = jnp.array([0, positions], jnp.int32)
        dummy = jnp.zeros((1, frames, width), BF16)
    gains = gains[:, None, :]

    def begin_position(v):
        return group.begin(jnp.moveaxis(v.reshape((mp, size) + v.shape[1:]), 1, 0))

    def end_position(keep, give):
        got = jnp.moveaxis(group.end(keep, give), 0, -3)
        return got.reshape(got.shape[:-3] + (rows, got.shape[-1]))

    def by_position(v):
        return end_position(*begin_position(v))

    normed_all, qkv, probs, context, attn_parts = [], [], [], [], []
    cot_own = [group.spread(chunk).reshape(rows, width) for chunk in cot_chunks]
    step = None
    for c in range(chunks):
        if not pair:
            own, other = every, dummy
        else:
            if c:
                other_blocks[c] = tied(step, other_blocks[c])[0]
            other = delayed_chunk(other_lags, other_earlier, other_blocks, c)
            own = resid[c]
            if c == 0:
                own, other, cot_own[c] = lax.optimization_barrier((own, other, cot_own[c]))
        *kept, own_part, other_part = attention_fwd(info, own, other, gains, w_qkv, w_out)
        step = own_part
        for held, array in zip((normed_all, qkv, probs, context), kept, strict=True):
            held.append(array)
        attn_parts.append((own_part, other_part))

    lines = [[o * size + k for o in range(outer)] for k in range(size)]

    def sum_lines(part):
        return lax.psum_scatter(
            part, "dp", scatter_dimension=0, axis_index_groups=lines, tiled=True
        )[0]

    middle, ffn_own, given = [], [], None
    for c in range(chunks):
        if pair:
            got = group.swap(attn_parts[c][1])
            if c:
                got = tied(given, got)[0]
            else:
                got, step = lax.optimization_barrier((got, step))
            whole = attn_parts[c][0] + got.astype(F32)
        else:
            whole = lax.psum_scatter(attn_parts[c][0], "mp", scatter_dimension=0, tiled=True)
        middle.append(resid[c].astype(F32) + whole)
        scale = lax.rsqrt(jnp.mean(middle[c] * middle[c], axis=-1, keepdims=True) + EPSILON)
        normed_f = (middle[c] * scale * ffn_gain[:, None, :]).astype(BF16)
        if pair and c == chunks - 1:
            last_normed_f = normed_f
            break
        keep, given = group.begin(normed_f)
        ffn_own.append(group.end(keep, given).reshape(rows, width))
    def feed(r, step, x_rows, g_rows, beside=(), between=()):
        position = jnp.asarray(group.index(r) * size + group.member, jnp.int32)
        kind = F32 if r == 0 or not pair else BF16
        results, moved = [], []
        for c in range(chunks):
            xs, gs = tied(step, x_rows[c], g_rows[c])
            if between and c:
                between = [by_position(v)[:, None] for v in tied(step, *between)]
                xs, *between = lax.optimization_barrier((xs, *between))
            if beside:
                keep, give = begin_position(beside[c])
                xs, give = lax.optimization_barrier((xs, give))
                moved.append(end_position(keep, give))
            result = ffn(position, xs, gs, w_gate_up, w_down, kind)
            step = result[0]
            if beside:
                step, moved[c] = lax.optimization_barrier((step, moved[c]))
                result = (step, *result[1:])
            results.append(result)
        return [list(v) for v in zip(*results, strict=True)], moved, list(between)

    blocks_of = lambda d_rows: d_rows.astype(BF16).reshape(size, part, width)

    def back_to_positions(d_normed_f, c):
        middle_grad, gain_part = norm_back(middle[c], ffn_gain, d_normed_f.astype(F32))
        return cot_chunks[c].astype(F32) + middle_grad, gain_part

    ffn_sums = []
    if pair:

        def own_positions(x_rows, last, g_rows):
            last = group.spread(last).reshape(rows, width)
            swapped = [group.swap(g_rows[0]), group.swap(x_rows)]
            (hidden, d_gate_up, d_own, out_own), _, _ = feed(0, x_rows, [x_rows, last], g_rows)
            hidden[1], *swapped = lax.optimization_barrier((hidden[1], *swapped))
            grad = ffn_grad(g_rows, [x_rows, last], hidden, d_gate_up, outer)
            return grad, last, swapped, d_own, out_own

        grad_own, last, (cot_other, ffn_other), d_own, out_own = region(
            item_bounds[0] >= 0, own_positions, ffn_own[0], last_normed_f, cot_own
        )
        ffn_sums.append(sum_lines(grad_own))

        def other_positions(x_first, g_first, x_last, g_last, d_own, normed, held):
            x_rows, g_rows = [x_first, group.swap(x_last)], [g_first, group.swap(g_last)]
            (hidden, d_gate_up, d_other, out_other), normed, held = feed(1, x_first, x_rows, g_rows, normed, held)
            got = [group.swap(block) for block in d_other]
            hidden[1], got[0] = lax.optimization_barrier((hidden[1], got[0]))
            keep, give = group.begin_back(blocks_of(d_own[0] + got[0].astype(F32)))
            hidden[0], give = lax.optimization_barrier((hidden[0], give))
            grad = ffn_grad(g_rows, x_rows, hidden, d_gate_up, outer)
            moved = group.first_back(give)
            grad, moved, got[1] = lax.optimization_barrier((grad, moved, got[1]))
            d_middle, gain_part = back_to_positions(group.end_back(keep, moved), 0)
            low = d_middle.astype(BF16)
            low, got[1] = lax.optimization_barrier((low, got[1]))
            d_first = group.swap(low)
            keep, give = group.begin_back(blocks_of(d_own[1] + got[1].astype(F32)))
            moved, d_first = lax.optimization_barrier((group.first_back(give), d_first))
            d_last = group.end_back(keep, moved)
            d_late, gain_late = back_to_positions(d_last, 1)
            d_middle = [d_middle, d_late]
            lows = [low, d_late.astype(BF16)]
            return grad, d_middle, lows, d_first, gain_part + gain_late, out_other, normed, held

        grad, d_middle, d_middle_low, d_first, ffn_gain_part, out_other, normed_rows, context_rows = region(
            item_bounds[0] >= 0,
            other_positions,
            ffn_other,
            cot_other,
            last,
            cot_own[1],
            d_own,
            normed_all,
            context,
        )
        out_parts = [out_own, out_other]
        ffn_sums[0], d_middle_low[1] = lax.optimization_barrier((ffn_sums[0], d_middle_low[1]))
        ffn_sums.append(sum_lines(tied(ffn_sums[0], grad)[0]))
    else:
        normed_rows = [by_position(normed_all[0])]
        context_rows = [by_position(context[0])[:, None]]
        cot_rows = [[block] for block in group.gather(cot_own[0])]
        ffn_rows = [[block] for block in group.gather(ffn_own[0])]
        d_parts, out_parts = [], []
        for r in range(mp):
            (hidden, d_gate_up, d_part, out_part), _, _ = feed(r, step, ffn_rows[r], cot_rows[r])
            d_parts.append(d_part[0])
            out_parts.append(out_part)
            step = ffn_grad(cot_rows[r], ffn_rows[r], hidden, d_gate_up, outer)
            ffn_sums.append(sum_lines(step))
        d_mid, ffn_gain_part = back_to_positions(group.unspread(blocks_of(group.scatter(d_parts))), 0)
        d_middle, d_middle_low = [d_mid], [d_mid.astype(BF16)]
        d_middle_all = [lax.all_gather(d_middle_low[0], "mp", axis=0, tiled=True)]
        d_middle_two = [[d_middle_all[0], dummy]]

    def finish(whole):
        depth, n = whole.shape[-2:]
        blocks = whole.reshape(whole.shape[:-2] + (size, depth // size, n))
        return group.in_order(group.spread(jnp.moveaxis(blocks, -3, 0)))

    def ffn_grads(done):
        done = jnp.stack(group.by_index(done)).astype(F32)
        done = done.reshape((positions,) + done.shape[2:])
        return done[:, 0], done[:, 1:]

    def ends(d_normed_a, out_rows, middle, d_middle, ffn_gain_part):
        mixed = []
        for c in range(chunks):
            got = group.unspread(blocks_of(out_rows[c]))
            mixed.append((middle[c] + got.astype(F32)).astype(BF16))
        mixed = jnp.concatenate(mixed, axis=1)

        d_resid, attn_gain_part = [], 0.0
        for c in range(chunks):
            resid_grad, gain_part = norm_back(resid[c].astype(F32), attn_gain, d_normed_a[c])
            attn_gain_part = attn_gain_part + gain_part
            d_resid.append(d_middle[c] + resid_grad)
        d_resid = jnp.concatenate(d_resid, axis=1)
        usable = frame_ids[None, :] - delays[:, None] >= item_start[None, :]
        spread = jnp.where(usable[:, :, None], d_resid, 0.0)
        one = (delays == 1)[:, None, None]
        blank = jnp.zeros((local_pos, 1, width), F32)
        head = spread[:, :2]
        placed = jnp.where(one, jnp.concatenate([blank, head[:, :1]], axis=1), head)
        returned = shift_frames(placed, -1)
        tail = jnp.concatenate([spread, blank, blank], axis=1)
        input_grad = jnp.where(one, tail[:, 1 : frames + 1], tail[:, 2:])
        input_grad = input_grad + jnp.pad(returned, ((0, 0), (frames - 2, 0), (0, 0)))
        gains = group.sum_scatter(jnp.stack([attn_gain_part, ffn_gain_part]))
        return mixed, input_grad, gains[0], gains[1]

    if pair:

        def attention_back(d_middle_low, d_first, qkv, probs, normed_rows, context_rows, out_other):
            d_last = group.swap(d_middle_low[1])
            two = [[d_middle_low[0], d_first], [d_middle_low[1], d_last]]
            keep, give = begin_position(jnp.concatenate(group.by_index(two[0])))
            *two[0], give = lax.optimization_barrier((*two[0], give))
            mid_first = end_position(keep, give)
            d_qkv, own_first, other_first = attention_bwd(info, *two[0], qkv[0], probs[0], w_qkv, w_out)
            d_qkv, mid_first, two[1][1] = lax.optimization_barrier((d_qkv, mid_first, two[1][1]))
            keep, give = begin_position(d_qkv)
            *two[1], give = lax.optimization_barrier((*two[1], give))
            d_later, own_last, other_last = attention_bwd(info, *two[1], qkv[1], probs[1], w_qkv, w_out)
            d_qkv = end_position(keep, give)
            sent = [group.swap(block) for block in out_other]
            d_later, d_qkv, sent[0] = lax.optimization_barrier((d_later, d_qkv, sent[0]))
            d_later = by_position(d_later)
            keep, give = begin_position(jnp.concatenate(group.by_index(two[1])))
            d_later, give = lax.optimization_barrier((d_later, give))
            mid_last = end_position(keep, give)
            qkv_part = weight_grad(normed_rows, [d_qkv, d_later], outer)
            qkv_part, mid_last, sent[1] = lax.optimization_barrier((qkv_part, mid_last, sent[1]))
            out_part = weight_grad([mid_first, mid_last], context_rows, outer)
            return qkv_part, out_part, [own_first, own_last], [other_first, other_last], sent

        qkv_part, out_part, own_parts, other_parts, sent = region(
            item_bounds[0] >= 0,
            attention_back,
            d_middle_low,
            d_first,
            qkv,
            probs,
            normed_rows,
            context_rows,
            out_parts[1],
        )
        ffn_sums[1], own_parts[0] = lax.optimization_barrier((ffn_sums[1], own_parts[0]))
        qkv_sums = sum_lines(tied(ffn_sums[1], qkv_part)[0])

        def others(own_parts, other_parts, out_own, sent, middle, d_middle, sums, gain_part):
            got = [group.swap(block) for block in other_parts]
            done = [finish(v) for v in sums]
            got[1], done[0] = lax.optimization_barrier((got[1], done[0]))
            done[1], gain_part = lax.optimization_barrier((done[1], gain_part))
            d_normed_a = [own_parts[c] + got[c].astype(F32) for c in range(chunks)]
            out_rows = [out_own[c] + sent[c].astype(F32) for c in range(chunks)]
            return ffn_grads(done), *ends(d_normed_a, out_rows, middle, d_middle, gain_part)

        (down_grad, gate_up_grad), mixed, input_grad, attn_gain_grad, ffn_gain_grad = region(
            item_bounds[0] >= 0,
            others,
            own_parts,
            other_parts,
            out_parts[0],
            sent,
            middle,
            d_middle,
            ffn_sums,
            ffn_gain_part,
        )
        qkv_sums, out_part, attn_gain_grad = lax.optimization_barrier((qkv_sums, out_part, attn_gain_grad))
        out_sums = sum_lines(out_part)
    else:
        d_qkv, own_part, _ = attention_bwd(info, *d_middle_two[0], qkv[0], probs[0], w_qkv, w_out)
        d_normed_a = [lax.psum_scatter(own_part, "mp", scatter_dimension=0, tiled=True)]
        out_part = weight_grad([by_position(d_middle_all[0])], context_rows, outer)
        qkv_part = weight_grad(normed_rows, [by_position(d_qkv)], outer)
        out_rows = [group.scatter([out_parts[r][0] for r in range(mp)])]
        qkv_sums, out_sums = sum_lines(qkv_part), sum_lines(out_part)
        down_grad, gate_up_grad = ffn_grads([finish(v) for v in ffn_sums])
        mixed, input_grad, attn_gain_grad, ffn_gain_grad = ends(
            d_normed_a, out_rows, middle, d_middle, ffn_gain_part
        )

    qkv_done = finish(qkv_sums)
    out_done = finish(tied(qkv_done, out_sums)[0])
    def both(got):
        got = jnp.swapaxes(got, 0, 1)
        return got.reshape((positions,) + got.shape[2:]).astype(F32)

    out_grad, qkv_grad = both(out_done)[:, 0], both(qkv_done)
    return (
        mixed,
        input_grad,
        attn_gain_grad,
        ffn_gain_grad,
        qkv_grad,
        out_grad,
        gate_up_grad,
        down_grad,
    )


def solution(mesh):
    placed = (
        P("mp", "dp", None),
        P("mp"),
        P(),
        P("mp", None),
        P("mp", None),
        P(None, None, None, "mp"),
        P(None, None, "mp"),
        P(None, None, None, "mp"),
        P(None, None, "mp"),
        P("mp", "dp", None),
    )
    return jax.shard_map(
        local,
        mesh=mesh,
        in_specs=placed,
        out_specs=(
            P("mp", "dp", None),
            P("mp", "dp", None),
            P("mp", "dp"),
            P("mp", "dp"),
            P(None, None, "dp", "mp"),
            P(None, "dp", "mp"),
            P(None, None, "dp", "mp"),
            P(None, "dp", "mp"),
        ),
        check_vma=False,
    )
```

```python
import functools

import jax
import jax.numpy as jnp
from jax import lax
from jax.experimental import pallas as pl
from jax.experimental.pallas import tpu as pltpu
from jax.sharding import PartitionSpec as P

HD = 64
LANES = 128
EPSILON = 1e-05
BF16 = jnp.bfloat16
F32 = jnp.float32
MIB = 1024 * 1024
WEIGHT = 100


def dot(left, right, contract):
    return lax.dot_general(left, right, ((contract[:1], contract[1:]), ((), ())), preferred_element_type=F32)


def shift_frames(block, distance):
    devices = range(lax.axis_size("dp"))
    route = [(i - distance, i) for i in devices if i - distance in devices]
    return lax.ppermute(block, "dp", route)


def at(array, index, axis=0):
    return lax.dynamic_index_in_dim(array, index, axis, keepdims=False)


def tied(first, *then):
    return lax.optimization_barrier((first, *then))[1:]


def region(ready, body, *operands):
    blank = lambda *_: jax.tree.map(lambda o: jnp.zeros(o.shape, o.dtype), jax.eval_shape(body, *operands))
    return lax.cond(ready, body, blank, *operands)


class Group:
    def __init__(self, local_pos):
        self.dp, self.mp = lax.axis_size("dp"), lax.axis_size("mp")
        power = local_pos & (local_pos - 1) == 0
        self.size = local_pos if power and self.dp % local_pos == 0 else 1
        self.outer = self.dp // self.size
        self.member = lax.axis_index("dp") % self.size
        self.m = lax.axis_index("mp")
        self.pair = self.mp == 2

    def index(self, r):
        return lax.rem(self.m + r, 2) if self.pair else r

    def swap(self, block):
        return lax.ppermute(block, "mp", [(0, 1), (1, 0)])

    def gather(self, block):
        if self.pair:
            return [block, self.swap(block)]
        every = lax.all_gather(block, "mp", axis=0)
        return [every[r] for r in range(self.mp)]

    def scatter(self, parts, after=None):
        if self.pair:
            got = self.swap(parts[1].astype(BF16))
            if after is not None:
                got = tied(after, got)[0]
            return parts[0].astype(F32) + got.astype(F32)
        return lax.psum_scatter(jnp.stack(parts).astype(F32), "mp", scatter_dimension=0, tiled=False)

    def by_index(self, parts):
        if self.pair:
            first = self.m == 0
            return [jnp.where(first, parts[0], parts[1]), jnp.where(first, parts[1], parts[0])]
        return parts

    def route(self, step):
        return [(i, i ^ step) for i in range(self.dp)]

    def begin(self, blocks):
        held, bit = blocks[:, None], 1
        while bit < self.size:
            halves = held.reshape((held.shape[0] // 2, 2) + held.shape[1:])
            side = jnp.where((self.member & bit) != 0, 1, 0)
            keep, give = at(halves, side, 1), at(halves, 1 - side, 1)
            if 2 * bit == self.size:
                return keep, give
            held = jnp.concatenate([keep, lax.ppermute(give, "dp", self.route(bit))], axis=1)
            bit *= 2
        return held, None

    def end(self, keep, give):
        if give is None:
            return keep[0]
        return jnp.concatenate([keep, lax.ppermute(give, "dp", self.route(self.size // 2))], axis=1)[0]

    def spread(self, blocks):
        return self.end(*self.begin(blocks))

    def begin_back(self, blocks):
        held, half = [blocks[s][None] for s in range(self.size)], self.size // 2
        return held, jnp.stack(held[half:]) if half else None

    def first_back(self, give):
        return give if give is None else lax.ppermute(give, "dp", self.route(self.size // 2))

    def end_back(self, held, got):
        bit = self.size // 2
        while bit:
            if got is None:
                got = lax.ppermute(jnp.stack(held[bit:]), "dp", self.route(bit))
            held, got = [jnp.concatenate([held[s], got[s]]) for s in range(bit)], None
            bit //= 2
        bits = self.size.bit_length() - 1
        turn = [int(format(s, "b").zfill(bits)[::-1] or "0", 2) for s in range(self.size)]
        return self.in_order([held[0][turn[s]] for s in range(self.size)])

    def unspread(self, blocks):
        held, give = self.begin_back(blocks)
        return self.end_back(held, self.first_back(give))

    def in_order(self, blocks):
        bit = 1
        while bit < self.size:
            odd = (self.member & bit) != 0
            blocks = [jnp.where(odd, blocks[s ^ bit], blocks[s]) for s in range(self.size)]
            bit *= 2
        return jnp.stack(blocks)

    def sum_scatter(self, values):
        if self.dp & (self.dp - 1):
            return lax.psum_scatter(values, "dp", scatter_dimension=values.ndim - 1, tiled=True)
        me, bit = lax.axis_index("dp"), self.dp // 2
        while bit:
            halves = values.reshape(values.shape[:-1] + (2, values.shape[-1] // 2))
            high = (me & bit) != 0
            keep = jnp.where(high, halves[..., 1, :], halves[..., 0, :])
            give = jnp.where(high, halves[..., 0, :], halves[..., 1, :])
            values = keep + lax.ppermute(give, "dp", self.route(bit))
            bit //= 2
        return values


def params(mib, **more):
    return pltpu.CompilerParams(vmem_limit_bytes=mib * MIB, **more)


def cost(flops, moved, weight):
    return pl.CostEstimate(flops=int(flops * weight), bytes_accessed=int(moved * weight), transcendentals=0)


def call(kernel, grid, args, in_specs, outs, out_specs, scratch, name, flops, prefetch=0, aliases={}, mib=48, weight=WEIGHT):
    moved = sum(a.size * a.dtype.itemsize for a in args) + sum(o.size * o.dtype.itemsize for o in outs)
    return pl.pallas_call(
        kernel,
        grid_spec=pltpu.PrefetchScalarGridSpec(
            num_scalar_prefetch=prefetch,
            grid=grid,
            in_specs=in_specs,
            out_specs=out_specs,
            scratch_shapes=scratch,
        ),
        out_shape=outs,
        input_output_aliases=aliases,
        compiler_params=params(mib),
        cost_estimate=cost(flops, moved, weight),
        name=name,
    )(*args)


def turned(rows, heads):
    return rows.T.reshape(heads, HD, rows.shape[0])


def per_head(scores):
    return scores[:, None, :]


def attention_fwd_kernel(
    heads, held, info, own, other, gain, w_qkv, w_out,
    normed_ref, qkv_ref, probs_ref, context_ref, own_ref, other_ref, keys, values, total
):
    p = pl.program_id(0)
    is_own = (p >= info[0]) & (p < info[0] + held)
    rows = jnp.where(is_own, own[0].astype(F32), other[0].astype(F32))
    scale = lax.rsqrt(jnp.mean(rows * rows, axis=-1, keepdims=True) + EPSILON)
    normed = (rows * scale * gain[0]).astype(BF16)
    normed_ref[0] = normed
    parts = []
    for c in range(3):
        low = turned(dot(normed, w_qkv[0, c], (1, 0)).astype(BF16), heads)
        qkv_ref[0, c] = low
        parts.append(low.astype(F32))
    query = parts[0] * 0.125
    keys[p], values[p] = parts[1], parts[2]
    probs_ref[...] = jnp.full(probs_ref.shape, -1e30, F32)

    def score(j, carry):
        probs_ref[0, j] = jnp.sum(query * keys[j], axis=1)
        return carry

    lax.fori_loop(0, p + 1, score, 0)
    scores = probs_ref[0]
    weights = jnp.exp(scores - jnp.max(scores, axis=0, keepdims=True))
    probs_ref[0] = weights / jnp.sum(weights, axis=0, keepdims=True)
    total[...] = jnp.zeros_like(total)

    def mix(j, carry):
        low = probs_ref[0, j].astype(BF16).astype(F32)
        total[...] += per_head(low) * values[j]
        return carry

    lax.fori_loop(0, p + 1, mix, 0)
    context = total[...].astype(BF16).reshape(heads * HD, -1).T
    context_ref[0] = context
    part = dot(context, w_out[0], (1, 1))

    @pl.when(is_own)
    def _():
        own_ref[0] = part

    @pl.when(jnp.logical_not(is_own))
    def _():
        other_ref[0] = part.astype(BF16)


def attention_fwd(info, own, other, gain, w_qkv, w_out):
    positions, _, width, head_width = w_qkv.shape
    heads = head_width // HD
    held, frames = own.shape[:2]
    rest = other.shape[0]
    block = lambda p, info: jnp.clip(p - info[0], 0, held - 1)
    away = lambda p, info: jnp.clip(p - info[1], 0, rest - 1)
    in_specs = [
        pl.BlockSpec((1, frames, width), lambda p, info: (block(p, info), 0, 0)),
        pl.BlockSpec((1, frames, width), lambda p, info: (away(p, info), 0, 0)),
        pl.BlockSpec((1, 1, width), lambda p, info: (p, 0, 0)),
        pl.BlockSpec((1, 3, width, head_width), lambda p, info: (p, 0, 0, 0)),
        pl.BlockSpec((1, width, head_width), lambda p, info: (p, 0, 0)),
    ]
    outs = [
        jax.ShapeDtypeStruct((positions, frames, width), BF16),
        jax.ShapeDtypeStruct((positions, 3, heads, HD, frames), BF16),
        jax.ShapeDtypeStruct((positions, positions, heads, frames), F32),
        jax.ShapeDtypeStruct((positions, frames, head_width), BF16),
        jax.ShapeDtypeStruct((held, frames, width), F32),
        jax.ShapeDtypeStruct((rest, frames, width), BF16),
    ]
    out_specs = [
        pl.BlockSpec((1, frames, width), lambda p, info: (p, 0, 0)),
        pl.BlockSpec((1, 3, heads, HD, frames), lambda p, info: (p, 0, 0, 0, 0)),
        pl.BlockSpec((1, positions, heads, frames), lambda p, info: (p, 0, 0, 0)),
        pl.BlockSpec((1, frames, head_width), lambda p, info: (p, 0, 0)),
        pl.BlockSpec((1, frames, width), lambda p, info: (block(p, info), 0, 0)),
        pl.BlockSpec((1, frames, width), lambda p, info: (away(p, info), 0, 0)),
    ]
    return call(
        functools.partial(attention_fwd_kernel, heads, held),
        (positions,),
        (info, own, other, gain, w_qkv, w_out),
        in_specs,
        outs,
        out_specs,
        [
            pltpu.VMEM((positions, heads, HD, frames), F32),
            pltpu.VMEM((positions, heads, HD, frames), F32),
            pltpu.VMEM((heads, HD, frames), F32),
        ],
        "attention_fwd",
        8 * positions * frames * width * head_width,
        prefetch=1,
    )


def attention_bwd_kernel(
    positions, heads, held, info, own, other, qkv, probs, w_qkv, w_out,
    d_qkv_ref, own_ref, other_ref, d_keys, d_values, d_query, d_scores
):
    step = pl.program_id(0)
    p = positions - 1 - step

    @pl.when(step == 0)
    def _():
        d_keys[...] = jnp.zeros_like(d_keys)
        d_values[...] = jnp.zeros_like(d_values)

    is_own = (p >= info[0]) & (p < info[0] + held)
    rows = jnp.where(is_own, own[0].astype(F32), other[0].astype(F32)).astype(BF16)
    d_context = turned(dot(rows, w_out[0], (1, 0)).astype(BF16), heads).astype(F32)
    d_scores[...] = jnp.zeros_like(d_scores)

    def weigh(j, carry):
        d_scores[j] = jnp.sum(d_context * qkv[j, 2].astype(F32), axis=1)
        d_values[j] += per_head(probs[0, j].astype(BF16).astype(F32)) * d_context
        return carry

    lax.fori_loop(0, p + 1, weigh, 0)
    prob, d_probs = probs[0], d_scores[...]
    d_scores[...] = (
        (prob * (d_probs - jnp.sum(prob * d_probs, axis=0, keepdims=True))).astype(BF16).astype(F32)
    ) * 0.125
    d_query[...] = jnp.zeros_like(d_query)
    query = qkv[p, 0].astype(F32)

    def back(j, carry):
        share = per_head(d_scores[j])
        d_query[...] += share * qkv[j, 1].astype(F32)
        d_keys[j] += share * query
        return carry

    lax.fori_loop(0, p + 1, back, 0)
    part = 0.0
    for c, grad in enumerate((d_query[...], d_keys[p], d_values[p])):
        low = grad.astype(BF16).reshape(heads * HD, -1).T
        d_qkv_ref[0, c] = low
        part = part + dot(low, w_qkv[0, c], (1, 1))

    @pl.when(is_own)
    def _():
        own_ref[0] = part

    @pl.when(jnp.logical_not(is_own))
    def _():
        other_ref[0] = part.astype(BF16)


def attention_bwd(info, own, other, qkv, probs, w_qkv, w_out):
    positions, _, width, head_width = w_qkv.shape
    heads = head_width // HD
    held, frames = own.shape[:2]
    rest = other.shape[0]
    back = lambda s: positions - 1 - s
    block = lambda s, info: jnp.clip(back(s) - info[0], 0, held - 1)
    away = lambda s, info: jnp.clip(back(s) - info[1], 0, rest - 1)
    return call(
        functools.partial(attention_bwd_kernel, positions, heads, held),
        (positions,),
        (info, own, other, qkv, probs, w_qkv, w_out),
        [
            pl.BlockSpec((1, frames, width), lambda s, info: (block(s, info), 0, 0)),
            pl.BlockSpec((1, frames, width), lambda s, info: (away(s, info), 0, 0)),
            pl.BlockSpec((positions, 3, heads, HD, frames), lambda s, info: (0, 0, 0, 0, 0)),
            pl.BlockSpec((1, positions, heads, frames), lambda s, info: (back(s), 0, 0, 0)),
            pl.BlockSpec((1, 3, width, head_width), lambda s, info: (back(s), 0, 0, 0)),
            pl.BlockSpec((1, width, head_width), lambda s, info: (back(s), 0, 0)),
        ],
        [
            jax.ShapeDtypeStruct((positions, 3, frames, head_width), BF16),
            jax.ShapeDtypeStruct((held, frames, width), F32),
            jax.ShapeDtypeStruct((rest, frames, width), BF16),
        ],
        [
            pl.BlockSpec((1, 3, frames, head_width), lambda s, info: (back(s), 0, 0, 0)),
            pl.BlockSpec((1, frames, width), lambda s, info: (block(s, info), 0, 0)),
            pl.BlockSpec((1, frames, width), lambda s, info: (away(s, info), 0, 0)),
        ],
        [
            pltpu.VMEM((positions, heads, HD, frames), F32),
            pltpu.VMEM((positions, heads, HD, frames), F32),
            pltpu.VMEM((heads, HD, frames), F32),
            pltpu.VMEM((positions, heads, frames), F32),
        ],
        "attention_bwd",
        8 * positions * frames * width * head_width,
        prefetch=1,
        mib=56,
    )


def ffn_kernel(info, rows, cot, w_up, w_down, hidden_ref, d_gate_up_ref, d_rows_ref, out_ref):
    gate = dot(rows[...], w_up[0, 0], (1, 0))
    up = dot(rows[...], w_up[0, 1], (1, 0))
    sigma = jax.nn.sigmoid(gate)
    silu = gate * sigma
    hidden = (silu * up).astype(BF16)
    hidden_ref[...] = hidden
    d_hidden = dot(cot[...], w_down[0], (1, 0))
    d_gate = (d_hidden * up * sigma * (1.0 + gate * (1.0 - sigma))).astype(BF16)
    d_up = (d_hidden * silu).astype(BF16)
    d_gate_up_ref[0], d_gate_up_ref[1] = d_gate, d_up
    d_rows = dot(d_gate, w_up[0, 0], (1, 1)) + dot(d_up, w_up[0, 1], (1, 1))
    d_rows_ref[...] = d_rows.astype(d_rows_ref.dtype)
    out_ref[...] = dot(hidden, w_down[0], (1, 1)).astype(out_ref.dtype)


def ffn(position, rows, cot, w_gate_up, w_down, kind):
    count, width = rows.shape
    units = w_down.shape[2]
    block = min(count, 512)
    row = lambda i, info: (i, 0)
    return call(
        ffn_kernel,
        (count // block,),
        (position.reshape(1), rows, cot, w_gate_up, w_down),
        [
            pl.BlockSpec((block, width), row),
            pl.BlockSpec((block, width), row),
            pl.BlockSpec((1, 2, width, units), lambda i, info: (info[0], 0, 0, 0)),
            pl.BlockSpec((1, width, units), lambda i, info: (info[0], 0, 0)),
        ],
        [
            jax.ShapeDtypeStruct((count, units), BF16),
            jax.ShapeDtypeStruct((2, count, units), BF16),
            jax.ShapeDtypeStruct((count, width), kind),
            jax.ShapeDtypeStruct((count, width), kind),
        ],
        [
            pl.BlockSpec((block, units), row),
            pl.BlockSpec((2, block, units), lambda i, info: (0, i, 0)),
            pl.BlockSpec((block, width), row),
            pl.BlockSpec((block, width), row),
        ],
        [],
        "feed_forward",
        12 * count * width * units,
        prefetch=1,
        mib=56,
    )


def weight_grad_kernel(count, *refs):
    lefts, rights, out = refs[:count], refs[count:-1], refs[-1]
    sums = 0.0
    for left, right in zip(lefts, rights, strict=True):
        sums = sums + dot(left[0], right[0, 0], (0, 0))
    out[0, 0, 0] = sums.astype(BF16)


def weight_grad(lefts, rights, outer):
    groups, rows, depth = lefts[0].shape
    parts, width = rights[0].shape[1], rights[0].shape[3]
    block = depth // outer
    if block % LANES:
        full = sum(
            jnp.einsum("grd,gcrn->gcdn", left, right, preferred_element_type=F32)
            for left, right in zip(lefts, rights, strict=True)
        )
        return full.astype(BF16).reshape(groups, parts, outer, block, width).transpose(2, 0, 1, 3, 4)
    count = len(lefts)
    return call(
        functools.partial(weight_grad_kernel, count),
        (groups, parts, outer),
        (*lefts, *rights),
        [pl.BlockSpec((1, rows, block), lambda g, c, o: (g, 0, o))] * count
        + [pl.BlockSpec((1, 1, rows, width), lambda g, c, o: (g, c, 0, 0))] * count,
        [jax.ShapeDtypeStruct((outer, groups, parts, block, width), BF16)],
        [pl.BlockSpec((1, 1, 1, block, width), lambda g, c, o: (o, g, c, 0, 0))],
        [],
        "weight_grad",
        2 * count * groups * parts * rows * depth * width,
    )[0]


def ffn_grad_kernel(count, *refs):
    cots, rows, hidden, d_gate_up = (refs[i * count : (i + 1) * count] for i in range(4))
    out = refs[-1]

    @pl.when(pl.program_id(0) == 0)
    def _():
        out[0, 0] = sum(dot(x[...], y[...], (0, 0)) for x, y in zip(cots, hidden, strict=True)).astype(BF16)

    @pl.when(pl.program_id(0) > 0)
    def _():
        out[0, 0] = sum(dot(x[...], y[0], (0, 0)) for x, y in zip(rows, d_gate_up, strict=True)).astype(BF16)


def ffn_grad(cots, rows, hidden, d_gate_up, outer):
    length, depth = cots[0].shape
    width = hidden[0].shape[1]
    block = depth // outer
    if block % LANES:
        first = sum(dot(x, y, (0, 0)) for x, y in zip(cots, hidden, strict=True))[None]
        others = sum(
            jnp.einsum("rd,crn->cdn", x, y, preferred_element_type=F32)
            for x, y in zip(rows, d_gate_up, strict=True)
        )
        full = jnp.concatenate([first, others]).astype(BF16)
        return full.reshape(3, outer, block, width).transpose(1, 0, 2, 3)
    count = len(cots)
    return call(
        functools.partial(ffn_grad_kernel, count),
        (3, outer),
        (*cots, *rows, *hidden, *d_gate_up),
        [pl.BlockSpec((length, block), lambda c, o: (0, jnp.where(c == 0, o, outer - 1)))] * count
        + [pl.BlockSpec((length, block), lambda c, o: (0, jnp.where(c == 0, 0, o)))] * count
        + [pl.BlockSpec((length, width), lambda c, o: (0, 0))] * count
        + [pl.BlockSpec((1, length, width), lambda c, o: (jnp.maximum(c - 1, 0), 0, 0))] * count,
        [jax.ShapeDtypeStruct((outer, 3, block, width), BF16)],
        [pl.BlockSpec((1, 1, block, width), lambda c, o: (o, c, 0, 0))],
        [],
        "ffn_grad",
        6 * count * length * depth * width,
    )[0]


def norm_back(values, gain, upstream):
    scale = lax.rsqrt(jnp.mean(values * values, axis=-1, keepdims=True) + EPSILON)
    gained = gain[:, None, :] * upstream
    gain_grad = jnp.sum(upstream * values * scale, axis=1)
    value_grad = scale * gained - values * (scale * scale * scale) * jnp.mean(
        gained * values, axis=-1, keepdims=True
    )
    return value_grad, gain_grad


def local(
    frames_in, delays, item_bounds, attn_gain, ffn_gain, w_qkv, w_out, w_gate_up, w_down, cotangent
):
    local_pos, frames, width = frames_in.shape
    positions, head_width = w_qkv.shape[0], w_qkv.shape[3]
    group = Group(local_pos)
    mp, size, outer, pair = group.mp, group.size, group.outer, group.pair
    chunks = 2 if pair and frames % 32 == 0 else 1
    part = frames // chunks

    frame_ids = lax.axis_index("dp") * frames + jnp.arange(frames, dtype=jnp.int32)
    item_start = jnp.where(
        frame_ids >= item_bounds[1],
        item_bounds[1],
        jnp.where(frame_ids >= item_bounds[0], item_bounds[0], 0),
    )

    def delayed(lags, before, block, c):
        padded = jnp.concatenate([before, block], axis=1)
        shifted = jnp.where((lags == 1)[:, None, None], padded[:, 1:-1], padded[:, :-2])
        usable = frame_ids[None, :] - lags[:, None] >= item_start[None, :]
        usable = usable[:, c * part : (c + 1) * part]
        return jnp.where(usable[:, :, None], shifted, jnp.zeros_like(shifted))

    def delayed_chunk(lags, earlier, blocks, c):
        return delayed(lags, blocks[c - 1][:, part - 2 :] if c else earlier, blocks[c], c)

    own_blocks = [frames_in[:, c * part : (c + 1) * part] for c in range(chunks)]
    rows = size * part
    *own_blocks, late_cotangent, last_two, own_gain = lax.optimization_barrier(
        (*own_blocks, cotangent, frames_in[:, frames - 2 :, :], attn_gain)
    )
    cot_chunks = [late_cotangent[:, c * part : (c + 1) * part] for c in range(chunks)]
    earlier = shift_frames(last_two, 1)
    resid = [delayed_chunk(delays, earlier, own_blocks, c) for c in range(chunks)]
    if pair:
        small = jnp.concatenate(
            [own_gain, jnp.broadcast_to(delays.astype(F32)[:, None], (local_pos, LANES))], axis=1
        )
        small = group.swap(small)
        other_blocks = []
        for block in own_blocks:
            if other_blocks:
                block = tied(other_blocks[-1], block)[0]
            other_blocks.append(group.swap(block))
        other_gain, other_lags = small[:, :width], small[:, width].astype(jnp.int32)
        other_earlier = group.swap(earlier)
        gains = jnp.concatenate(group.by_index([attn_gain, other_gain]))
        first, second = group.m * local_pos, (1 - group.m) * local_pos
        info = jnp.stack([first, second]).astype(jnp.int32)
    else:
        gains = lax.all_gather(attn_gain, "mp", axis=0, tiled=True)
        every = lax.all_gather(resid[0], "mp", axis=0, tiled=True)
        info = jnp.array([0, positions], jnp.int32)
        dummy = jnp.zeros((1, frames, width), BF16)
    gains = gains[:, None, :]

    def begin_position(v):
        return group.begin(jnp.moveaxis(v.reshape((mp, size) + v.shape[1:]), 1, 0))

    def end_position(keep, give):
        got = jnp.moveaxis(group.end(keep, give), 0, -3)
        return got.reshape(got.shape[:-3] + (rows, got.shape[-1]))

    def by_position(v):
        return end_position(*begin_position(v))

    normed_all, qkv, probs, context, attn_parts = [], [], [], [], []
    cot_own = [group.spread(chunk).reshape(rows, width) for chunk in cot_chunks]
    step = None
    for c in range(chunks):
        if not pair:
            own, other = every, dummy
        else:
            if c:
                other_blocks[c] = tied(step, other_blocks[c])[0]
            other = delayed_chunk(other_lags, other_earlier, other_blocks, c)
            own = resid[c]
            if c == 0:
                own, other, cot_own[c] = lax.optimization_barrier((own, other, cot_own[c]))
        *kept, own_part, other_part = attention_fwd(info, own, other, gains, w_qkv, w_out)
        step = own_part
        for held, array in zip((normed_all, qkv, probs, context), kept, strict=True):
            held.append(array)
        attn_parts.append((own_part, other_part))

    lines = [[o * size + k for o in range(outer)] for k in range(size)]

    def sum_lines(part):
        return lax.psum_scatter(
            part, "dp", scatter_dimension=0, axis_index_groups=lines, tiled=True
        )[0]

    middle, ffn_own, given = [], [], None
    for c in range(chunks):
        if pair:
            got = group.swap(attn_parts[c][1])
            if c:
                got = tied(given, got)[0]
            else:
                got, step = lax.optimization_barrier((got, step))
            whole = attn_parts[c][0] + got.astype(F32)
        else:
            whole = lax.psum_scatter(attn_parts[c][0], "mp", scatter_dimension=0, tiled=True)
        middle.append(resid[c].astype(F32) + whole)
        scale = lax.rsqrt(jnp.mean(middle[c] * middle[c], axis=-1, keepdims=True) + EPSILON)
        normed_f = (middle[c] * scale * ffn_gain[:, None, :]).astype(BF16)
        if pair and c == chunks - 1:
            last_normed_f = normed_f
            break
        keep, given = group.begin(normed_f)
        ffn_own.append(group.end(keep, given).reshape(rows, width))
    def feed(r, step, x_rows, g_rows, beside=(), between=()):
        position = jnp.asarray(group.index(r) * size + group.member, jnp.int32)
        kind = F32 if r == 0 or not pair else BF16
        results, moved = [], []
        for c in range(chunks):
            xs, gs = tied(step, x_rows[c], g_rows[c])
            if between and c:
                between = [by_position(v)[:, None] for v in tied(step, *between)]
                xs, *between = lax.optimization_barrier((xs, *between))
            if beside:
                keep, give = begin_position(beside[c])
                xs, give = lax.optimization_barrier((xs, give))
                moved.append(end_position(keep, give))
            result = ffn(position, xs, gs, w_gate_up, w_down, kind)
            step = result[0]
            if beside:
                step, moved[c] = lax.optimization_barrier((step, moved[c]))
                result = (step, *result[1:])
            results.append(result)
        return [list(v) for v in zip(*results, strict=True)], moved, list(between)

    blocks_of = lambda d_rows: d_rows.astype(BF16).reshape(size, part, width)

    def back_to_positions(d_normed_f, c):
        middle_grad, gain_part = norm_back(middle[c], ffn_gain, d_normed_f.astype(F32))
        return cot_chunks[c].astype(F32) + middle_grad, gain_part

    ffn_sums = []
    if pair:

        def own_positions(x_rows, last, g_rows):
            last = group.spread(last).reshape(rows, width)
            swapped = [group.swap(g_rows[0]), group.swap(x_rows)]
            (hidden, d_gate_up, d_own, out_own), _, _ = feed(0, x_rows, [x_rows, last], g_rows)
            hidden[1], *swapped = lax.optimization_barrier((hidden[1], *swapped))
            grad = ffn_grad(g_rows, [x_rows, last], hidden, d_gate_up, outer)
            return grad, last, swapped, d_own, out_own

        grad_own, last, (cot_other, ffn_other), d_own, out_own = region(
            item_bounds[0] >= 0, own_positions, ffn_own[0], last_normed_f, cot_own
        )
        ffn_sums.append(sum_lines(grad_own))

        def other_positions(x_first, g_first, x_last, g_last, d_own, normed, held):
            x_rows, g_rows = [x_first, group.swap(x_last)], [g_first, group.swap(g_last)]
            (hidden, d_gate_up, d_other, out_other), normed, held = feed(1, x_first, x_rows, g_rows, normed, held)
            got = [group.swap(block) for block in d_other]
            hidden[1], got[0] = lax.optimization_barrier((hidden[1], got[0]))
            keep, give = group.begin_back(blocks_of(d_own[0] + got[0].astype(F32)))
            hidden[0], give = lax.optimization_barrier((hidden[0], give))
            grad = ffn_grad(g_rows, x_rows, hidden, d_gate_up, outer)
            moved = group.first_back(give)
            grad, moved, got[1] = lax.optimization_barrier((grad, moved, got[1]))
            d_middle, gain_part = back_to_positions(group.end_back(keep, moved), 0)
            low = d_middle.astype(BF16)
            low, got[1] = lax.optimization_barrier((low, got[1]))
            d_first = group.swap(low)
            keep, give = group.begin_back(blocks_of(d_own[1] + got[1].astype(F32)))
            moved, d_first = lax.optimization_barrier((group.first_back(give), d_first))
            d_last = group.end_back(keep, moved)
            d_late, gain_late = back_to_positions(d_last, 1)
            d_middle = [d_middle, d_late]
            lows = [low, d_late.astype(BF16)]
            return grad, d_middle, lows, d_first, gain_part + gain_late, out_other, normed, held

        grad, d_middle, d_middle_low, d_first, ffn_gain_part, out_other, normed_rows, context_rows = region(
            item_bounds[0] >= 0,
            other_positions,
            ffn_other,
            cot_other,
            last,
            cot_own[1],
            d_own,
            normed_all,
            context,
        )
        out_parts = [out_own, out_other]
        ffn_sums[0], d_middle_low[1] = lax.optimization_barrier((ffn_sums[0], d_middle_low[1]))
        ffn_sums.append(sum_lines(tied(ffn_sums[0], grad)[0]))
    else:
        normed_rows = [by_position(normed_all[0])]
        context_rows = [by_position(context[0])[:, None]]
        cot_rows = [[block] for block in group.gather(cot_own[0])]
        ffn_rows = [[block] for block in group.gather(ffn_own[0])]
        d_parts, out_parts = [], []
        for r in range(mp):
            (hidden, d_gate_up, d_part, out_part), _, _ = feed(r, step, ffn_rows[r], cot_rows[r])
            d_parts.append(d_part[0])
            out_parts.append(out_part)
            step = ffn_grad(cot_rows[r], ffn_rows[r], hidden, d_gate_up, outer)
            ffn_sums.append(sum_lines(step))
        d_mid, ffn_gain_part = back_to_positions(group.unspread(blocks_of(group.scatter(d_parts))), 0)
        d_middle, d_middle_low = [d_mid], [d_mid.astype(BF16)]
        d_middle_all = [lax.all_gather(d_middle_low[0], "mp", axis=0, tiled=True)]
        d_middle_two = [[d_middle_all[0], dummy]]

    def finish(whole):
        depth, n = whole.shape[-2:]
        blocks = whole.reshape(whole.shape[:-2] + (size, depth // size, n))
        return group.in_order(group.spread(jnp.moveaxis(blocks, -3, 0)))

    def ffn_grads(done):
        done = jnp.stack(group.by_index(done)).astype(F32)
        done = done.reshape((positions,) + done.shape[2:])
        return done[:, 0], done[:, 1:]

    def ends(d_normed_a, out_rows, middle, d_middle, ffn_gain_part):
        mixed = []
        for c in range(chunks):
            got = group.unspread(blocks_of(out_rows[c]))
            mixed.append((middle[c] + got.astype(F32)).astype(BF16))
        mixed = jnp.concatenate(mixed, axis=1)

        d_resid, attn_gain_part = [], 0.0
        for c in range(chunks):
            resid_grad, gain_part = norm_back(resid[c].astype(F32), attn_gain, d_normed_a[c])
            attn_gain_part = attn_gain_part + gain_part
            d_resid.append(d_middle[c] + resid_grad)
        d_resid = jnp.concatenate(d_resid, axis=1)
        usable = frame_ids[None, :] - delays[:, None] >= item_start[None, :]
        spread = jnp.where(usable[:, :, None], d_resid, 0.0)
        one = (delays == 1)[:, None, None]
        blank = jnp.zeros((local_pos, 1, width), F32)
        head = spread[:, :2]
        placed = jnp.where(one, jnp.concatenate([blank, head[:, :1]], axis=1), head)
        returned = shift_frames(placed, -1)
        tail = jnp.concatenate([spread, blank, blank], axis=1)
        input_grad = jnp.where(one, tail[:, 1 : frames + 1], tail[:, 2:])
        input_grad = input_grad + jnp.pad(returned, ((0, 0), (frames - 2, 0), (0, 0)))
        gains = group.sum_scatter(jnp.stack([attn_gain_part, ffn_gain_part]))
        return mixed, input_grad, gains[0], gains[1]

    if pair:

        def attention_back(d_middle_low, d_first, qkv, probs, normed_rows, context_rows, out_other):
            d_last = group.swap(d_middle_low[1])
            two = [[d_middle_low[0], d_first], [d_middle_low[1], d_last]]
            keep, give = begin_position(jnp.concatenate(group.by_index(two[0])))
            *two[0], give = lax.optimization_barrier((*two[0], give))
            mid_first = end_position(keep, give)
            d_qkv, own_first, other_first = attention_bwd(info, *two[0], qkv[0], probs[0], w_qkv, w_out)
            d_qkv, mid_first, two[1][1] = lax.optimization_barrier((d_qkv, mid_first, two[1][1]))
            keep, give = begin_position(d_qkv)
            *two[1], give = lax.optimization_barrier((*two[1], give))
            d_later, own_last, other_last = attention_bwd(info, *two[1], qkv[1], probs[1], w_qkv, w_out)
            d_qkv = end_position(keep, give)
            sent = [group.swap(block) for block in out_other]
            d_later, d_qkv, sent[0] = lax.optimization_barrier((d_later, d_qkv, sent[0]))
            d_later = by_position(d_later)
            keep, give = begin_position(jnp.concatenate(group.by_index(two[1])))
            d_later, give = lax.optimization_barrier((d_later, give))
            mid_last = end_position(keep, give)
            qkv_part = weight_grad(normed_rows, [d_qkv, d_later], outer)
            qkv_part, mid_last, sent[1] = lax.optimization_barrier((qkv_part, mid_last, sent[1]))
            out_part = weight_grad([mid_first, mid_last], context_rows, outer)
            return qkv_part, out_part, [own_first, own_last], [other_first, other_last], sent

        qkv_part, out_part, own_parts, other_parts, sent = region(
            item_bounds[0] >= 0,
            attention_back,
            d_middle_low,
            d_first,
            qkv,
            probs,
            normed_rows,
            context_rows,
            out_parts[1],
        )
        ffn_sums[1], own_parts[0] = lax.optimization_barrier((ffn_sums[1], own_parts[0]))
        qkv_sums = sum_lines(tied(ffn_sums[1], qkv_part)[0])

        def others(own_parts, other_parts, out_own, sent, middle, d_middle, sums, gain_part):
            got = [group.swap(block) for block in other_parts]
            done = [finish(v) for v in sums]
            got[1], done[0] = lax.optimization_barrier((got[1], done[0]))
            done[1], gain_part = lax.optimization_barrier((done[1], gain_part))
            d_normed_a = [own_parts[c] + got[c].astype(F32) for c in range(chunks)]
            out_rows = [out_own[c] + sent[c].astype(F32) for c in range(chunks)]
            return ffn_grads(done), *ends(d_normed_a, out_rows, middle, d_middle, gain_part)

        (down_grad, gate_up_grad), mixed, input_grad, attn_gain_grad, ffn_gain_grad = region(
            item_bounds[0] >= 0,
            others,
            own_parts,
            other_parts,
            out_parts[0],
            sent,
            middle,
            d_middle,
            ffn_sums,
            ffn_gain_part,
        )
        qkv_sums, out_part, attn_gain_grad = lax.optimization_barrier((qkv_sums, out_part, attn_gain_grad))
        out_sums = sum_lines(out_part)
    else:
        d_qkv, own_part, _ = attention_bwd(info, *d_middle_two[0], qkv[0], probs[0], w_qkv, w_out)
        d_normed_a = [lax.psum_scatter(own_part, "mp", scatter_dimension=0, tiled=True)]
        out_part = weight_grad([by_position(d_middle_all[0])], context_rows, outer)
        qkv_part = weight_grad(normed_rows, [by_position(d_qkv)], outer)
        out_rows = [group.scatter([out_parts[r][0] for r in range(mp)])]
        qkv_sums, out_sums = sum_lines(qkv_part), sum_lines(out_part)
        down_grad, gate_up_grad = ffn_grads([finish(v) for v in ffn_sums])
        mixed, input_grad, attn_gain_grad, ffn_gain_grad = ends(
            d_normed_a, out_rows, middle, d_middle, ffn_gain_part
        )

    qkv_done = finish(qkv_sums)
    out_done = finish(tied(qkv_done, out_sums)[0])
    def both(got):
        got = jnp.swapaxes(got, 0, 1)
        return got.reshape((positions,) + got.shape[2:]).astype(F32)

    out_grad, qkv_grad = both(out_done)[:, 0], both(qkv_done)
    return (
        mixed,
        input_grad,
        attn_gain_grad,
        ffn_gain_grad,
        qkv_grad,
        out_grad,
        gate_up_grad,
        down_grad,
    )


def solution(mesh):
    placed = (
        P("mp", "dp", None),
        P("mp"),
        P(),
        P("mp", None),
        P("mp", None),
        P(None, None, None, "mp"),
        P(None, None, "mp"),
        P(None, None, None, "mp"),
        P(None, None, "mp"),
        P("mp", "dp", None),
    )
    return jax.shard_map(
        local,
        mesh=mesh,
        in_specs=placed,
        out_specs=(
            P("mp", "dp", None),
            P("mp", "dp", None),
            P("mp", "dp"),
            P("mp", "dp"),
            P(None, None, "dp", "mp"),
            P(None, "dp", "mp"),
            P(None, None, "dp", "mp"),
            P(None, "dp", "mp"),
        ),
        check_vma=False,
    )
```
